32 devices in a mesh: dp: 16 (over z, y, x), mp: 2 (over core).
Axes of the slice: x: 2, y: 2, z: 4, core: 2. Of those that a mesh axis runs over, the one named last changes fastest.
Arguments:
- layer_input: bfloat16 [8192, 8192], P('dp', 'mp')
- norm_gain: bfloat16 [8192], P('mp'), may hold values from 0.5 to 1.5
- value_weight: bfloat16 [1024, 8192], P('dp', 'mp'), may hold values from -0.0625 to 0.0625
- value_cotangent: bfloat16 [8192, 1024], P('dp', 'mp')
- doc_ids: int32 [8192], P('dp'), may hold values from 0 to 31, never falling along the last dimension, each value on 1 to 512 neighbouring positions
- owners: int32 [16], replicated, may hold values from 0 to 15, as said below
- noise_seeds: int32 [16], replicated, may hold values from 0 to 1073741823
- master: float32 [4096, 8192], P('dp', 'mp'), may hold values from -0.12 to 0.12
- moment_one: float32 [4096, 8192], P('dp', 'mp'), may hold values from -6 to 6
- moment_two: float32 [4096, 8192], P('dp', 'mp'), may hold values from 0.5 to 8
Outputs:
- input_grad: bfloat16 [8192, 8192], P('dp', 'mp')
- new_master: float32 [4096, 8192], P('dp', 'mp')
- new_moment_one: float32 [4096, 8192], P('dp', 'mp')
- new_moment_two: float32 [4096, 8192], P('dp', 'mp')
The draws below stay inside these ranges and needn't reach their ends.
Inputs may be any that keep to these rules, and one draw needn't show every extreme that they name: `owners`: each index of dp is named by at most 4 entries, and one is named by exactly 4.
All inputs are finite; a program needn't handle non-finite values.
Results may differ from the reference program's by a relative error of at most 0.0016.
Values may be sent and summed in bfloat16 or wider, within the bound.
A program may use at most 128 MiB of HBM per device.

```python
import math
import jax
import jax.numpy as jnp
import numpy as np
from jax import lax

D = 8192
KV = 1024
TOK_DEV = 512
CAP = 4
TOKENS = 8192
GROUP_ROWS = 64
N_DP = 16


def draw_layer_input(key, part):
    key = jax.random.fold_in(key, 3)
    key_noise, key_common, key_spread = jax.random.split(key, 3)
    columns = jnp.arange(D, dtype=jnp.float32) / D
    noise_part = jax.random.normal(key_noise, (TOKENS, D), jnp.float32)
    shared = 0.6
    common = jax.random.normal(key_common, (1, D), jnp.float32)
    spread = jax.random.uniform(key_spread, (1, D), jnp.float32)
    scales = jnp.exp(jnp.log(10.0) * (0.5 * columns + 0.5 * spread))
    return ((noise_part + shared * common) * scales).astype(jnp.bfloat16)


def draw_value_cotangent(key, part):
    key = jax.random.fold_in(key, 5)
    key_noise, key_common, key_rows = jax.random.split(key, 3)
    noise_part = jax.random.normal(key_noise, (TOKENS, KV), jnp.float32)
    shared = 0.6
    reach = jnp.log(10.0)
    common = jax.random.normal(key_common, (1, KV), jnp.float32)
    row_scale = jnp.exp(reach * jax.random.uniform(key_rows, (TOKENS, 1), jnp.float32))
    return ((noise_part + shared * common) * row_scale).astype(jnp.bfloat16)


def draw_owners(key, part):
    key = jax.random.fold_in(key, 11)
    key_order, key_offset = jax.random.split(key)
    shuffled = jax.random.permutation(key_order, N_DP).astype(jnp.int32)
    groups = jnp.arange(N_DP, dtype=jnp.int32)
    offsets = jax.random.randint(key_offset, (N_DP,), 0, CAP).astype(jnp.int32)
    offsets = jnp.where(groups < CAP, groups, offsets)
    buckets = jnp.mod(groups - offsets, N_DP).astype(jnp.int32)
    return shuffled[buckets].astype(jnp.int32)


def plant(values, rng, low, top_value):
    spot = [jax.random.randint(jax.random.fold_in(rng, axis), (), 0, length) for axis, length in enumerate(values.shape)]
    widest = values.shape.index(max(values.shape))
    neighbour = spot[:widest] + [(spot[widest] + 1) % values.shape[widest]] + spot[widest + 1:]
    return values.at[tuple(spot)].set(low).at[tuple(neighbour)].set(top_value)


def block_scale(own_key, extent, cuts, least, largest):
    level = 1.0
    for dim, shards_of in cuts:
        draws = jax.random.uniform(jax.random.fold_in(jax.random.fold_in(own_key, 6), dim), (shards_of,), jnp.float32, least / len(cuts), largest / len(cuts))
        level = level * jnp.repeat(jnp.exp(draws), extent[dim] // shards_of).reshape((-1,) + (1,) * (len(extent) - 1 - dim))
    return level


def length_profile(number_of, total, most, skew):
    portions = [(1 << 20) // math.isqrt(grade ** skew) + 1 for grade in range(2, number_of + 1)]
    surplus, given = total - most - (number_of - 1), [1] * (number_of - 1)
    while surplus > 0:
        movable = [i for i in range(number_of - 1) if given[i] < most]
        whole, left = sum([portions[i] for i in movable]), surplus
        for i in movable:
            extra = min(most - given[i], max(1, left * portions[i] // whole), surplus)
            given[i] = given[i] + extra
            surplus = surplus - extra
    return np.array([most] + given)


def ragged(key, amount, total, most, slope):
    if amount == 2:
        one = jax.random.randint(key, (), max(1, total - most), min(most, total - 1) + 1)
        return jnp.stack([one, total - one])
    lengths = jnp.asarray(length_profile(amount, total, most, slope), jnp.int32)
    couples = (amount - 1) // 2
    giver, taker = lengths[1:1 + 2 * couples:2], lengths[2:2 + 2 * couples:2]
    room = jnp.minimum(giver - 1, most - taker)
    shifted = jax.random.randint(jax.random.fold_in(key, 1), (couples,), 0, 1 << 20) % (room + 1)
    lengths = lengths.at[1:1 + 2 * couples:2].set(giver - shifted).at[2:2 + 2 * couples:2].set(taker + shifted)
    return lengths[jax.random.permutation(jax.random.fold_in(key, 2), amount)]


def centred(key, dims, scale, bound, cuts=(), held_as=jnp.bfloat16):
    gain = block_scale(key, dims, cuts, -0.22, 0.18) if cuts else 1.0
    drawn = jax.random.normal(key, dims, jnp.float32) * scale * gain
    return jnp.minimum(jnp.maximum(drawn, -bound), bound).astype(held_as)


def setup_inputs(seed: int = 0) -> dict:
    streams_of = jax.random.split(jax.random.key(seed), 11)
    return {
        "layer_input": draw_layer_input(jax.random.fold_in(streams_of[10], 71), 0),
        "norm_gain": jnp.clip(1.0 + 0.1 * jax.random.normal(streams_of[1], (D,), jnp.float32), 0.5, 1.5).astype(jnp.bfloat16),
        "value_weight": centred(streams_of[2], (KV, D), D ** -0.5, 0.0625, ((0, 16), (1, 2))),
        "value_cotangent": draw_value_cotangent(jax.random.fold_in(streams_of[10], 71), 0),
        "doc_ids": jnp.searchsorted(jnp.cumsum(ragged(streams_of[4], 2 * N_DP, TOKENS, TOK_DEV, 2)), jnp.arange(TOKENS), side="right").astype(jnp.int32),
        "owners": draw_owners(jax.random.fold_in(streams_of[10], 71), 0),
        "noise_seeds": plant(jax.random.randint(streams_of[6], (N_DP,), 0, 2**30), jax.random.fold_in(streams_of[6], 1), 0, (2**30) - 1).astype(jnp.int32),
        "master": centred(streams_of[7], (CAP * KV, D), 0.02, 0.12, ((0, 16), (1, 2)), jnp.float32),
        "moment_one": centred(streams_of[8], (CAP * KV, D), 1.0, 6.0, ((0, 16), (1, 2)), jnp.float32),
        "moment_two": jnp.clip(jnp.exp(math.log(8.0) - 2.7725887 * jax.random.uniform(streams_of[9], (CAP * KV, D), jnp.float32) ** block_scale(streams_of[9], (CAP * KV, D), ((0, 16), (1, 2)), -0.2, 0.2)), 0.5, 8.0),
    }


EPS_NORM = 1e-06
CLIP_NORM = 128.0
NOISE_MULT = 0.01
LEARN_RATE = 0.001
BETA_ONE = 0.9
BETA_TWO = 0.999
ADAM_STEP = 100
ADAM_EPS = 1e-08

def mix_bits(bits_in):
    bits_in = jnp.bitwise_xor(bits_in, lax.shift_right_logical(bits_in, jnp.int32(16)))
    bits_in = bits_in * jnp.int32(2146121005)
    bits_in = jnp.bitwise_xor(bits_in, lax.shift_right_logical(bits_in, jnp.int32(15)))
    bits_in = bits_in * jnp.int32(-2073254261)
    bits_in = jnp.bitwise_xor(bits_in, lax.shift_right_logical(bits_in, jnp.int32(16)))
    return bits_in

def unit_draw(seed_value, position):
    hashed = mix_bits(mix_bits(jnp.bitwise_xor(position, seed_value)) + seed_value)
    return (lax.shift_right_logical(hashed, jnp.int32(8)).astype(jnp.float32) + 0.5) * (1.0 / 16777216.0)

def gauss_noise(seed_value, position):
    draw_one = unit_draw(seed_value, 2 * position)
    draw_two = unit_draw(seed_value, 2 * position + 1)
    return jnp.sqrt(-2.0 * jnp.log(draw_one)) * jnp.cos(6.283185307179586 * draw_two)

def reference(layer_input, norm_gain, value_weight, value_cotangent, doc_ids, owners, noise_seeds, master, moment_one, moment_two):
    inputs = layer_input.astype(jnp.float32)
    gain_row = norm_gain.astype(jnp.float32)
    inv_rms = lax.rsqrt(lax.optimization_barrier(jnp.mean(inputs * inputs, axis=1, keepdims=True)) + EPS_NORM)
    normed = (inputs * inv_rms * gain_row).astype(jnp.bfloat16)
    dnormed = jnp.dot(value_cotangent, value_weight, preferred_element_type=jnp.float32)
    weighted = gain_row * dnormed
    inner_sum = lax.optimization_barrier(jnp.sum(weighted * inputs, axis=1, keepdims=True)) / D
    input_grad = (inv_rms * weighted - inputs * inv_rms * inv_rms * inv_rms * inner_sum).astype(jnp.bfloat16)
    normed_seqs = normed.reshape(N_DP, TOK_DEV, D)
    cot_seqs = value_cotangent.reshape(N_DP, TOK_DEV, KV)
    doc_seqs = doc_ids.reshape(N_DP, TOK_DEV)

    def seq_scale(seq_block):
        normed_block, cot_block, doc_block = seq_block
        gram_features = jnp.dot(normed_block, normed_block.T, preferred_element_type=jnp.float32)
        gram_values = jnp.dot(cot_block, cot_block.T, preferred_element_type=jnp.float32)
        same_doc = (doc_block[:, None] == doc_block[None, :]).astype(jnp.float32)
        row_sums = lax.optimization_barrier(jnp.sum(same_doc * gram_features * gram_values, axis=1))
        squared = jnp.dot(same_doc, row_sums, precision=lax.Precision.HIGHEST)
        return CLIP_NORM / (jnp.sqrt(squared) + 0.01)
    scales = lax.map(seq_scale, (normed_seqs, cot_seqs, doc_seqs)).reshape(TOKENS, 1)
    clipped = (value_cotangent.astype(jnp.float32) * scales).astype(jnp.bfloat16)
    weight_grad = lax.dot_general(clipped, normed, (((0,), (0,)), ((), ())), preferred_element_type=jnp.float32)
    row_idx = jnp.arange(KV, dtype=jnp.int32)
    col_idx = jnp.arange(D, dtype=jnp.int32)
    positions = (row_idx % GROUP_ROWS)[:, None] * D + col_idx[None, :]
    row_seeds = noise_seeds[row_idx // GROUP_ROWS][:, None]
    noisy = weight_grad + NOISE_MULT * CLIP_NORM * gauss_noise(row_seeds, positions)
    group_ids = jnp.arange(N_DP, dtype=jnp.int32)
    earlier = group_ids[:, None] > group_ids[None, :]
    same_owner = owners[:, None] == owners[None, :]
    slot_rank = lax.optimization_barrier(jnp.sum((earlier & same_owner).astype(jnp.int32), axis=1))
    targets = (owners * CAP + slot_rank).astype(jnp.int32)
    noisy_groups = noisy.reshape(N_DP, GROUP_ROWS, D)
    master_slots = master.reshape(N_DP * CAP, GROUP_ROWS, D)
    first_slots = moment_one.reshape(N_DP * CAP, GROUP_ROWS, D)
    second_slots = moment_two.reshape(N_DP * CAP, GROUP_ROWS, D)
    first_new = BETA_ONE * first_slots[targets] + (1.0 - BETA_ONE) * noisy_groups
    second_new = BETA_TWO * second_slots[targets] + (1.0 - BETA_TWO) * noisy_groups * noisy_groups
    update = first_new / (1.0 - BETA_ONE ** ADAM_STEP) / (jnp.sqrt(second_new / (1.0 - BETA_TWO ** ADAM_STEP)) + ADAM_EPS)
    master_new = master_slots[targets] - LEARN_RATE * update
    new_master = master_slots.at[targets].set(master_new).reshape(CAP * KV, D)
    new_moment_one = first_slots.at[targets].set(first_new).reshape(CAP * KV, D)
    new_moment_two = second_slots.at[targets].set(second_new).reshape(CAP * KV, D)
    return (input_grad, new_master, new_moment_one, new_moment_two)
```

```python
import functools

import jax
import jax.numpy as jnp
from jax import lax
from jax.experimental import pallas as pl
from jax.experimental.pallas import tpu as pltpu
from jax.sharding import PartitionSpec as P

EPS_NORM = 1e-06
CLIP_NORM = 128.0
NOISE_MULT = 0.01
LEARN_RATE = 0.001
BETA_ONE = 0.9
BETA_TWO = 0.999
ADAM_STEP = 100
ADAM_EPS = 1e-08


def mix_bits(bits_in):
    bits_in = jnp.bitwise_xor(bits_in, lax.shift_right_logical(bits_in, jnp.int32(16)))
    bits_in = bits_in * jnp.int32(2146121005)
    bits_in = jnp.bitwise_xor(bits_in, lax.shift_right_logical(bits_in, jnp.int32(15)))
    bits_in = bits_in * jnp.int32(-2073254261)
    bits_in = jnp.bitwise_xor(bits_in, lax.shift_right_logical(bits_in, jnp.int32(16)))
    return bits_in


def unit_draw(seed_value, position):
    hashed = mix_bits(mix_bits(jnp.bitwise_xor(position, seed_value)) + seed_value)
    return (lax.shift_right_logical(hashed, jnp.int32(8)).astype(jnp.float32) + 0.5) * (
        1.0 / 16777216.0
    )


def gauss_noise(seed_value, position):
    draw_one = unit_draw(seed_value, 2 * position)
    draw_two = unit_draw(seed_value, 2 * position + 1)
    return jnp.sqrt(-2.0 * jnp.log(draw_one)) * jnp.cos(6.283185307179586 * draw_two)


PLANE = 4


class Links:
    def __init__(self, planes):
        self.planes = planes
        me = lax.axis_index("dp")
        self.mp = lax.axis_index("mp")
        self.line = me // PLANE
        self.row = (me // 2) % 2
        self.col = me % 2

    def index(self, line, row, col):
        return line * PLANE + row * 2 + col

    def col_peer(self):
        return (self.index(self.line, self.row, 1 - self.col), self.mp)

    def row_peer(self):
        return (self.index(self.line, 1 - self.row, self.col), self.mp)

    def above(self):
        return (self.index(self.line + 1, self.row, self.col), self.mp)

    def below(self):
        return (self.index(self.line - 1, self.row, self.col), self.mp)

    def has_above(self):
        return self.line + 1 < self.planes

    def has_below(self):
        return self.line > 0

    def greet(self):
        barrier = pltpu.get_barrier_semaphore()
        mesh_ids = pl.DeviceIdType.MESH
        for peer in (self.col_peer(), self.row_peer()):
            pl.semaphore_signal(barrier, inc=1, device_id=peer, device_id_type=mesh_ids)

        @pl.when(self.has_above())
        def _():
            pl.semaphore_signal(barrier, inc=1, device_id=self.above(), device_id_type=mesh_ids)

        @pl.when(self.has_below())
        def _():
            pl.semaphore_signal(barrier, inc=1, device_id=self.below(), device_id_type=mesh_ids)

        ends = jnp.where(self.line > 0, 1, 0) + jnp.where(self.line + 1 < self.planes, 1, 0)
        pl.semaphore_wait(barrier, 2 + ends)


def remote(src, dst, send_sem, recv_sem, peer):
    return pltpu.make_async_remote_copy(
        src_ref=src,
        dst_ref=dst,
        send_sem=send_sem,
        recv_sem=recv_sem,
        device_id=peer,
        device_id_type=pl.DeviceIdType.MESH,
    )


def gather_kernel(planes, tile_ref, out_ref, own_sem, send_sems, recv_sems):
    links = Links(planes)
    half = tile_ref.shape[1] // 2
    mine = links.index(links.line, links.row, links.col)
    own = pltpu.make_async_copy(tile_ref, out_ref.at[mine], own_sem)
    own.start()
    links.greet()
    ways = (links.col_peer(), links.row_peer(), links.above(), links.below())
    pending = []

    def piece(shard, part):
        return out_ref.at[shard, :, pl.ds(part * half, half)]

    def transfer(shard, part, way, from_tile=False):
        source = tile_ref.at[:, pl.ds(part * half, half)] if from_tile else piece(shard, part)
        return remote(
            source,
            piece(shard, part),
            send_sems.at[shard, part, way],
            recv_sems.at[shard, part],
            ways[way],
        )

    def start(shard, part, way, guard, from_tile=False):
        copy = transfer(shard, part, way, from_tile)
        pending.append((guard, copy))
        if guard is None:
            copy.start()
        else:
            pl.when(guard)(copy.start)

    def arrive(shard, part, guard):
        copy = transfer(shard, part, 0)
        if guard is None:
            copy.wait_recv()
        else:
            pl.when(guard)(copy.wait_recv)

    def both(first, second):
        return second if first is None else jnp.logical_and(first, second)

    def spread(line, guard, from_tile):
        shard = links.index(line, links.row, links.col)
        start(shard, 0, 0, guard, from_tile)
        start(shard, 1, 1, guard, from_tile)
        start(shard, 0, 1, guard, from_tile)
        start(shard, 1, 0, guard, from_tile)

    def relay(line, guard):
        shard = links.index(line, links.row, 1 - links.col)
        arrive(shard, 0, guard)
        start(shard, 0, 1, guard)
        shard = links.index(line, 1 - links.row, links.col)
        arrive(shard, 1, guard)
        start(shard, 1, 0, guard)

    for part in (0, 1):
        start(mine, part, 2, links.has_above(), True)
        start(mine, part, 3, links.has_below(), True)
    spread(links.line, None, True)
    lines = [[(links.line, None)]]
    for step in range(1, planes):
        from_below = links.line - step
        from_above = links.line + step
        got_below = from_below >= 0
        got_above = from_above < planes
        for part in (0, 1):
            shard = links.index(from_below, links.row, links.col)
            arrive(shard, part, got_below)
            start(shard, part, 2, both(got_below, links.has_above()))
            shard = links.index(from_above, links.row, links.col)
            arrive(shard, part, got_above)
            start(shard, part, 3, both(got_above, links.has_below()))
        spread(from_below, got_below, False)
        spread(from_above, got_above, False)
        for line, guard in lines[-1]:
            relay(line, guard)
        lines.append([(from_below, got_below), (from_above, got_above)])
    for line, guard in lines[-1]:
        relay(line, guard)
    for group in lines:
        for line, guard in group:
            for part in (0, 1):
                arrive(links.index(line, 1 - links.row, 1 - links.col), part, guard)
            arrive(links.index(line, 1 - links.row, links.col), 0, guard)
            arrive(links.index(line, links.row, 1 - links.col), 1, guard)
    for guard, copy in pending:
        if guard is None:
            copy.wait_send()
        else:
            pl.when(guard)(copy.wait_send)
    own.wait()


def gather_tiles(tile, count):
    rows, width = tile.shape
    return pl.pallas_call(
        functools.partial(gather_kernel, count // PLANE),
        out_shape=jax.ShapeDtypeStruct((count, rows, width), tile.dtype),
        in_specs=[pl.BlockSpec(memory_space=pl.ANY)],
        out_specs=pl.BlockSpec(memory_space=pl.ANY),
        scratch_shapes=[
            pltpu.SemaphoreType.DMA,
            pltpu.SemaphoreType.DMA((count, 2, 4)),
            pltpu.SemaphoreType.DMA((count, 2)),
        ],
        compiler_params=pltpu.CompilerParams(collective_id=1, has_side_effects=True),
        cost_estimate=pl.CostEstimate(
            flops=0, bytes_accessed=2 * count * rows * width * 2, transcendentals=0
        ),
    )(tile)


def scatter_kernel(
    planes,
    part_ref,
    out_ref,
    first_in,
    second_in,
    line_in,
    second_out,
    line_out,
    send_sems,
    first_sems,
    second_sems,
    line_sems,
):
    links = Links(planes)
    rows, width = out_ref.shape
    half = width // 2
    block = 16
    links.greet()
    pending = []
    row, col, place = links.row, links.col, links.line
    order = sorted(range(planes), key=lambda line: -max(line, planes - 1 - line))
    first_peer = (links.row_peer(), links.col_peer())
    second_peer = (links.col_peer(), links.row_peer())

    def columns(part):
        return pl.ds(part * half, half)

    def first_copy(line, part):
        if part == 0:
            source = part_ref.at[line, 1 - row, :, :, columns(0)]
        else:
            source = part_ref.at[line, :, 1 - col, :, columns(1)]
        return remote(
            source,
            first_in.at[line, part],
            send_sems.at[line, part, 0],
            first_sems.at[line, part],
            first_peer[part],
        )

    def second_copy(line, part):
        return remote(
            second_out.at[line, part],
            second_in.at[line, part],
            send_sems.at[line, part, 1],
            second_sems.at[line, part],
            second_peer[part],
        )

    def line_copy(line, part, side):
        return remote(
            line_out.at[line, part],
            line_in.at[side, line, part],
            send_sems.at[line, part, 2],
            line_sems.at[side, line, part],
            links.above() if side == 0 else links.below(),
        )

    def send_first(line):
        for part in (0, 1):
            copy = first_copy(line, part)
            copy.start()
            pending.append((None, copy))

    def by_blocks(step):
        def at(index, carry):
            step(pl.ds(pl.multiple_of(index * block, block), block))
            return carry

        lax.fori_loop(0, rows // block, at, 0)

    def send_second(line):
        for part in (0, 1):
            first_copy(line, part).wait_recv()
            give_row, give_col = (row, 1 - col) if part == 0 else (1 - row, col)
            lane = 1 - col if part == 0 else 1 - row

            def step(at):
                second_out[line, part, at, :] = (
                    part_ref[line, give_row, give_col, at, columns(part)].astype(jnp.float32)
                    + first_in[line, part, lane, at, :].astype(jnp.float32)
                ).astype(jnp.bfloat16)

            by_blocks(step)
            copy = second_copy(line, part)
            copy.start()
            pending.append((None, copy))

    def plane_sum(line, part, at):
        lane = col if part == 0 else row
        return (
            part_ref[line, row, col, at, columns(part)].astype(jnp.float32)
            + first_in[line, part, lane, at, :].astype(jnp.float32)
            + second_in[line, part, at, :].astype(jnp.float32)
        )

    def send_line(line):
        for part in (0, 1):
            second_copy(line, part).wait_recv()

            @pl.when(place == line)
            def _():
                def step(at):
                    out_ref[at, columns(part)] = plane_sum(line, part, at)

                by_blocks(step)

            for side, sends, joins in (
                (0, place < line, place > 0),
                (1, place > line, place < planes - 1),
            ):

                @pl.when(jnp.logical_and(sends, joins))
                def _():
                    line_copy(line, part, side).wait_recv()

                    def step(at):
                        line_out[line, part, at, :] = (
                            plane_sum(line, part, at)
                            + line_in[side, line, part, at, :].astype(jnp.float32)
                        ).astype(jnp.bfloat16)

                    by_blocks(step)

                @pl.when(jnp.logical_and(sends, jnp.logical_not(joins)))
                def _():
                    def step(at):
                        line_out[line, part, at, :] = plane_sum(line, part, at).astype(jnp.bfloat16)

                    by_blocks(step)

                copy = line_copy(line, part, side)
                pl.when(sends)(copy.start)
                pending.append((sends, copy))

    ahead = 2
    for line in order[:ahead]:
        send_first(line)
    for index, line in enumerate(order):
        send_second(line)
        if index + ahead < planes:
            send_first(order[index + ahead])
        if index > 0:
            send_line(order[index - 1])
    send_line(order[-1])

    for side, joins in ((0, place > 0), (1, place < planes - 1)):
        for part in (0, 1):

            @pl.when(joins)
            def _():
                line_copy(place, part, side).wait_recv()

                def step(at):
                    out_ref[at, columns(part)] += line_in[side, place, part, at, :].astype(
                        jnp.float32
                    )

                by_blocks(step)

    for guard, copy in pending:
        if guard is None:
            copy.wait_send()
        else:
            pl.when(guard)(copy.wait_send)


def scatter_sum(partial_tiles, count):
    planes = count // PLANE
    rows = partial_tiles.shape[0] // count
    width = partial_tiles.shape[1]
    half = width // 2
    return pl.pallas_call(
        functools.partial(scatter_kernel, planes),
        out_shape=jax.ShapeDtypeStruct((rows, width), jnp.float32),
        in_specs=[pl.BlockSpec(memory_space=pltpu.VMEM)],
        out_specs=pl.BlockSpec(memory_space=pltpu.VMEM),
        scratch_shapes=[
            pltpu.VMEM((planes, 2, 2, rows, half), jnp.bfloat16),
            pltpu.VMEM((planes, 2, rows, half), jnp.bfloat16),
            pltpu.VMEM((2, planes, 2, rows, half), jnp.bfloat16),
            pltpu.VMEM((planes, 2, rows, half), jnp.bfloat16),
            pltpu.VMEM((planes, 2, rows, half), jnp.bfloat16),
            pltpu.SemaphoreType.DMA((planes, 2, 3)),
            pltpu.SemaphoreType.DMA((planes, 2)),
            pltpu.SemaphoreType.DMA((planes, 2)),
            pltpu.SemaphoreType.DMA((2, planes, 2)),
        ],
        compiler_params=pltpu.CompilerParams(
            collective_id=2, has_side_effects=True, vmem_limit_bytes=40 * 1024 * 1024
        ),
        cost_estimate=pl.CostEstimate(
            flops=4 * count * rows * width,
            bytes_accessed=8 * count * rows * width,
            transcendentals=0,
        ),
    )(partial_tiles.reshape(planes, 2, 2, rows, width))


def body(
    layer_input,
    norm_gain,
    value_weight,
    value_cotangent,
    doc_ids,
    owners,
    noise_seeds,
    master,
    moment_one,
    moment_two,
):
    part_width = layer_input.shape[1]
    full_width = part_width * lax.axis_size("mp")
    group_rows = value_weight.shape[0]
    slot_count = master.shape[0] // group_rows
    cycle_size = lax.axis_size("dp")
    my_group = lax.axis_index("dp")
    my_column = lax.axis_index("mp")
    inputs = layer_input.astype(jnp.float32)
    gain_row = norm_gain.astype(jnp.float32)
    squares = lax.psum(jnp.sum(inputs * inputs, axis=1), "mp")
    inv_rms = lax.rsqrt(squares / full_width + EPS_NORM)[:, None]
    normed = (inputs * inv_rms * gain_row).astype(jnp.bfloat16)
    seed_value = noise_seeds[my_group]
    row_pos = jnp.arange(group_rows, dtype=jnp.int32)[:, None]
    col_pos = my_column * part_width + jnp.arange(part_width, dtype=jnp.int32)[None, :]
    positions = row_pos * full_width + col_pos
    noise = lax.optimization_barrier(NOISE_MULT * CLIP_NORM * gauss_noise(seed_value, positions))
    full_weight = lax.all_gather(value_weight, "dp", axis=0, tiled=True)
    full_cot = lax.all_gather(value_cotangent, "mp", axis=1, tiled=True)
    same_doc = (doc_ids[:, None] == doc_ids[None, :]).astype(jnp.float32)
    gram_part = jnp.dot(normed, normed.T, preferred_element_type=jnp.float32)
    gram_values = jnp.dot(full_cot, full_cot.T, preferred_element_type=jnp.float32)
    gram_features = lax.psum(gram_part, "mp")
    mine_sums = jnp.sum(same_doc * gram_features * gram_values, axis=1)
    squared = jnp.dot(same_doc, mine_sums, precision=lax.Precision.HIGHEST)
    scales = CLIP_NORM / (jnp.sqrt(squared) + 0.01)
    clipped = (full_cot.astype(jnp.float32) * scales[:, None]).astype(jnp.bfloat16)
    group_ids = jnp.arange(cycle_size, dtype=jnp.int32)
    earlier = group_ids[:, None] > group_ids[None, :]
    same_owner = owners[:, None] == owners[None, :]
    slot_rank = jnp.sum((earlier & same_owner).astype(jnp.int32), axis=1)
    slot_ids = jnp.arange(slot_count, dtype=jnp.int32)
    holds_slot = (owners[None, :] == my_group) & (slot_rank[None, :] == slot_ids[:, None])
    sources = jnp.sum(jnp.where(holds_slot, group_ids[None, :], 0), axis=1)
    filled = jnp.any(holds_slot, axis=1)
    filled_rows = jnp.repeat(filled, group_rows)
    partial_grad = lax.dot_general(
        clipped, normed, (((0,), (0,)), ((), ())), preferred_element_type=jnp.float32
    ).astype(jnp.bfloat16)
    grad_tile = scatter_sum(partial_grad, cycle_size)
    noisy_tile = (grad_tile + noise).astype(jnp.bfloat16)
    arrived = gather_tiles(noisy_tile, cycle_size)
    late_cot, arrived = lax.optimization_barrier((full_cot, arrived))
    dnormed = jnp.dot(late_cot, full_weight, preferred_element_type=jnp.float32)
    weighted = gain_row * dnormed
    inner_sum = lax.psum(jnp.sum(weighted * inputs, axis=1), "mp")
    input_grad = (
        inv_rms * weighted
        - inputs * inv_rms * inv_rms * inv_rms * (inner_sum / full_width)[:, None]
    ).astype(jnp.bfloat16)
    gathered = jnp.take(arrived, sources, axis=0).reshape(slot_count * group_rows, part_width)
    gathered = gathered.astype(jnp.float32)
    first_new = BETA_ONE * moment_one + (1.0 - BETA_ONE) * gathered
    second_new = BETA_TWO * moment_two + (1.0 - BETA_TWO) * gathered * gathered
    update = (
        first_new
        / (1.0 - BETA_ONE**ADAM_STEP)
        / (jnp.sqrt(second_new / (1.0 - BETA_TWO**ADAM_STEP)) + ADAM_EPS)
    )
    master_new = master - LEARN_RATE * update
    keep_mask = filled_rows[:, None]
    new_master = jnp.where(keep_mask, master_new, master)
    new_moment_one = jnp.where(keep_mask, first_new, moment_one)
    new_moment_two = jnp.where(keep_mask, second_new, moment_two)
    return (input_grad, new_master, new_moment_one, new_moment_two)


def solution(mesh):
    in_specs = (
        P("dp", "mp"),
        P("mp"),
        P("dp", "mp"),
        P("dp", "mp"),
        P("dp"),
        P(),
        P(),
        P("dp", "mp"),
        P("dp", "mp"),
        P("dp", "mp"),
    )
    out_specs = (P("dp", "mp"), P("dp", "mp"), P("dp", "mp"), P("dp", "mp"))
    return jax.shard_map(body, mesh=mesh, in_specs=in_specs, out_specs=out_specs, check_vma=False)
```

```python
import functools

import jax
import jax.numpy as jnp
from jax import lax
from jax.experimental import pallas as pl
from jax.experimental.pallas import tpu as pltpu
from jax.sharding import PartitionSpec as P

EPS_NORM = 1e-06
CLIP_NORM = 128.0
NOISE_MULT = 0.01
LEARN_RATE = 0.001
BETA_ONE = 0.9
BETA_TWO = 0.999
ADAM_STEP = 100
ADAM_EPS = 1e-08


def mix_bits(bits_in):
    bits_in = jnp.bitwise_xor(bits_in, lax.shift_right_logical(bits_in, jnp.int32(16)))
    bits_in = bits_in * jnp.int32(2146121005)
    bits_in = jnp.bitwise_xor(bits_in, lax.shift_right_logical(bits_in, jnp.int32(15)))
    bits_in = bits_in * jnp.int32(-2073254261)
    bits_in = jnp.bitwise_xor(bits_in, lax.shift_right_logical(bits_in, jnp.int32(16)))
    return bits_in


def unit_draw(seed_value, position):
    hashed = mix_bits(mix_bits(jnp.bitwise_xor(position, seed_value)) + seed_value)
    return (lax.shift_right_logical(hashed, jnp.int32(8)).astype(jnp.float32) + 0.5) * (
        1.0 / 16777216.0
    )


def gauss_noise(seed_value, position):
    draw_one = unit_draw(seed_value, 2 * position)
    draw_two = unit_draw(seed_value, 2 * position + 1)
    return jnp.sqrt(-2.0 * jnp.log(draw_one)) * jnp.cos(6.283185307179586 * draw_two)


PLANE = 4


class Links:
    def __init__(self, planes):
        self.planes = planes
        me = lax.axis_index("dp")
        self.mp = lax.axis_index("mp")
        self.me = me
        self.cores = lax.axis_size("mp")
        self.line = me // PLANE
        self.row = (me // 2) % 2
        self.col = me % 2

    def index(self, line, row, col):
        return line * PLANE + row * 2 + col

    def col_peer(self):
        return (self.index(self.line, self.row, 1 - self.col), self.mp)

    def row_peer(self):
        return (self.index(self.line, 1 - self.row, self.col), self.mp)

    def above(self):
        return (self.index(self.line + 1, self.row, self.col), self.mp)

    def below(self):
        return (self.index(self.line - 1, self.row, self.col), self.mp)

    def has_above(self):
        return self.line + 1 < self.planes

    def has_below(self):
        return self.line > 0

    def core_peer(self, step):
        return (self.me, (self.mp + step) % self.cores)

    def greet_cores(self):
        barrier = pltpu.get_barrier_semaphore()
        for step in range(1, self.cores):
            pl.semaphore_signal(
                barrier,
                inc=1,
                device_id=self.core_peer(step),
                device_id_type=pl.DeviceIdType.MESH,
            )
        pl.semaphore_wait(barrier, self.cores - 1)

    def greet(self, with_cores=False):
        barrier = pltpu.get_barrier_semaphore()
        mesh_ids = pl.DeviceIdType.MESH
        for peer in (self.col_peer(), self.row_peer()):
            pl.semaphore_signal(barrier, inc=1, device_id=peer, device_id_type=mesh_ids)

        @pl.when(self.has_above())
        def _():
            pl.semaphore_signal(barrier, inc=1, device_id=self.above(), device_id_type=mesh_ids)

        @pl.when(self.has_below())
        def _():
            pl.semaphore_signal(barrier, inc=1, device_id=self.below(), device_id_type=mesh_ids)

        ends = jnp.where(self.line > 0, 1, 0) + jnp.where(self.line + 1 < self.planes, 1, 0)
        others = 0
        if with_cores:
            others = self.cores - 1
            for step in range(1, self.cores):
                pl.semaphore_signal(
                    barrier, inc=1, device_id=self.core_peer(step), device_id_type=mesh_ids
                )
        pl.semaphore_wait(barrier, 2 + others + ends)


def remote(src, dst, send_sem, recv_sem, peer):
    return pltpu.make_async_remote_copy(
        src_ref=src,
        dst_ref=dst,
        send_sem=send_sem,
        recv_sem=recv_sem,
        device_id=peer,
        device_id_type=pl.DeviceIdType.MESH,
    )


def clip_kernel(
    normed_ref, cot_ref, doc_col_ref, doc_row_ref, full_ref, clipped_ref, grams, send_sems, recv_sems
):
    links = Links(1)
    me, cores = links.mp, links.cores
    tokens, width = cot_ref.shape
    block = tokens // 2
    links.greet_cores()

    def cot_slot(core):
        return full_ref.at[:, pl.ds(pl.multiple_of(core * width, width), width)]

    def cot_copy(core, step):
        return remote(
            cot_ref,
            cot_slot(core),
            send_sems.at[step - 1, 0],
            recv_sems.at[core, 0],
            links.core_peer(step),
        )

    def gram_copy(core, step, part):
        rows = pl.ds(part * block, block)
        return remote(
            grams.at[core, rows],
            grams.at[core, rows],
            send_sems.at[step - 1, 1 + part],
            recv_sems.at[core, 1 + part],
            links.core_peer(step),
        )

    steps = range(1, cores)
    for step in steps:
        cot_copy(me, step).start()
    full_ref[:, pl.ds(pl.multiple_of(me * width, width), width)] = cot_ref[...]
    for part in range(2):
        grams[me, pl.ds(part * block, block), :] = lax.dot_general(
            normed_ref[pl.ds(part * block, block), :],
            normed_ref[...],
            (((1,), (1,)), ((), ())),
            preferred_element_type=jnp.float32,
        )
        for step in steps:
            gram_copy(me, step, part).start()
    for step in steps:
        cot_copy((me + step) % cores, step).wait_recv()
    gram_values = lax.dot_general(
        full_ref[...],
        full_ref[...],
        (((1,), (1,)), ((), ())),
        preferred_element_type=jnp.float32,
    )
    same_doc = doc_col_ref[...] == doc_row_ref[...]
    for step in steps:
        for part in range(2):
            gram_copy((me + step) % cores, step, part).wait_recv()
    gram_features = grams[0]
    for core in range(1, cores):
        gram_features = gram_features + grams[core]
    product = jnp.where(same_doc, gram_features * gram_values, 0.0)
    row_sums = jnp.sum(product, axis=0, keepdims=True)
    squared = jnp.sum(jnp.where(same_doc, row_sums, 0.0), axis=1, keepdims=True)
    scales = CLIP_NORM / (jnp.sqrt(squared) + 0.01)
    clipped_ref[...] = (full_ref[...].astype(jnp.float32) * scales).astype(jnp.bfloat16)
    for step in steps:
        cot_copy(me, step).wait_send()
        for part in range(2):
            gram_copy(me, step, part).wait_send()


def clip_by_document(normed, cot, doc_ids):
    tokens, width = cot.shape
    cores = lax.axis_size("mp")
    vmem = pl.BlockSpec(memory_space=pltpu.VMEM)
    full = jax.ShapeDtypeStruct((tokens, width * cores), cot.dtype)
    return pl.pallas_call(
        clip_kernel,
        out_shape=(full, full),
        in_specs=[vmem] * 4,
        out_specs=(vmem, vmem),
        scratch_shapes=[
            pltpu.VMEM((cores, tokens, tokens), jnp.float32),
            pltpu.SemaphoreType.DMA((cores - 1, 3)),
            pltpu.SemaphoreType.DMA((cores, 3)),
        ],
        compiler_params=pltpu.CompilerParams(
            collective_id=3, has_side_effects=True, vmem_limit_bytes=40 * 1024 * 1024
        ),
        cost_estimate=pl.CostEstimate(
            flops=2 * tokens * tokens * (normed.shape[1] + width * cores),
            bytes_accessed=2 * tokens * (normed.shape[1] + 4 * width * cores),
            transcendentals=0,
        ),
    )(normed, cot, doc_ids[:, None], doc_ids[None, :])


def gather_kernel(
    planes,
    tile_ref,
    weight_hbm,
    cot_ref,
    input_ref,
    gain_ref,
    inv_ref,
    out_ref,
    grad_ref,
    weight_ref,
    weighted_ref,
    inner_ref,
    own_sem,
    weight_sem,
    send_sems,
    recv_sems,
    inner_send,
    inner_recv,
):
    links = Links(planes)
    core, cores = links.mp, links.cores
    width = input_ref.shape[1]
    tile = width // 8
    fetch = pltpu.make_async_copy(weight_hbm, weight_ref, weight_sem)
    fetch.start()
    half = tile_ref.shape[1] // 2
    mine = links.index(links.line, links.row, links.col)
    own = pltpu.make_async_copy(tile_ref, out_ref.at[mine], own_sem)
    own.start()
    links.greet(True)

    def inner_copy(slot, step):
        return remote(
            inner_ref.at[slot],
            inner_ref.at[slot],
            inner_send.at[step - 1],
            inner_recv.at[slot],
            links.core_peer(step),
        )

    def project(low, high):
        def at(index, carry):
            columns = pl.ds(pl.multiple_of(index * tile, tile), tile)
            weighted = gain_ref[:, columns] * jnp.dot(
                cot_ref[...], weight_ref[:, columns], preferred_element_type=jnp.float32
            )
            weighted_ref[:, columns] = weighted
            product = weighted * input_ref[:, columns].astype(jnp.float32)
            total = inner_ref[core]
            for lane in range(tile // 128):
                total = total + product[:, lane * 128 : (lane + 1) * 128]
            inner_ref[core] = total
            return carry

        lax.fori_loop(low, high, at, 0)

    def project_first():
        inner_ref[core] = jnp.zeros(inner_ref.shape[1:], jnp.float32)
        fetch.wait()
        project(0, 4)

    def project_rest():
        project(4, 8)
        for step in range(1, cores):
            inner_copy(core, step).start()

    def inner_done():
        for step in range(1, cores):
            inner_copy((core + step) % cores, step).wait_recv()
        total = inner_ref[0]
        for slot in range(1, cores):
            total = total + inner_ref[slot]
        inner = jnp.sum(total, axis=1, keepdims=True) / (width * cores)
        inv = inv_ref[...]
        factor = inv * inv * inv * inner

        def at(index, carry):
            columns = pl.ds(pl.multiple_of(index * tile, tile), tile)
            grad_ref[:, columns] = (
                inv * weighted_ref[:, columns] - input_ref[:, columns].astype(jnp.float32) * factor
            ).astype(jnp.bfloat16)
            return carry

        lax.fori_loop(0, 8, at, 0)

    chores = [project_first, project_rest, inner_done]

    def chore():
        if chores:
            chores.pop(0)()

    ways = (links.col_peer(), links.row_peer(), links.above(), links.below())
    pending = []

    def piece(shard, part):
        return out_ref.at[shard, :, pl.ds(part * half, half)]

    def transfer(shard, part, way, from_tile=False):
        source = tile_ref.at[:, pl.ds(part * half, half)] if from_tile else piece(shard, part)
        return remote(
            source,
            piece(shard, part),
            send_sems.at[shard, part, way],
            recv_sems.at[shard, part],
            ways[way],
        )

    def start(shard, part, way, guard, from_tile=False):
        copy = transfer(shard, part, way, from_tile)
        pending.append((guard, copy))
        if guard is None:
            copy.start()
        else:
            pl.when(guard)(copy.start)

    def arrive(shard, part, guard):
        copy = transfer(shard, part, 0)
        if guard is None:
            copy.wait_recv()
        else:
            pl.when(guard)(copy.wait_recv)

    def both(first, second):
        return second if first is None else jnp.logical_and(first, second)

    def spread(line, guard, from_tile):
        shard = links.index(line, links.row, links.col)
        start(shard, 0, 0, guard, from_tile)
        start(shard, 1, 1, guard, from_tile)
        start(shard, 0, 1, guard, from_tile)
        start(shard, 1, 0, guard, from_tile)

    def relay(line, guard):
        shard = links.index(line, links.row, 1 - links.col)
        arrive(shard, 0, guard)
        start(shard, 0, 1, guard)
        shard = links.index(line, 1 - links.row, links.col)
        arrive(shard, 1, guard)
        start(shard, 1, 0, guard)

    for part in (0, 1):
        start(mine, part, 2, links.has_above(), True)
        start(mine, part, 3, links.has_below(), True)
    spread(links.line, None, True)
    chore()
    lines = [[(links.line, None)]]
    for step in range(1, planes):
        from_below = links.line - step
        from_above = links.line + step
        got_below = from_below >= 0
        got_above = from_above < planes
        for part in (0, 1):
            shard = links.index(from_below, links.row, links.col)
            arrive(shard, part, got_below)
            start(shard, part, 2, both(got_below, links.has_above()))
            shard = links.index(from_above, links.row, links.col)
            arrive(shard, part, got_above)
            start(shard, part, 3, both(got_above, links.has_below()))
        spread(from_below, got_below, False)
        spread(from_above, got_above, False)
        for line, guard in lines[-1]:
            relay(line, guard)
        chore()
        lines.append([(from_below, got_below), (from_above, got_above)])
    for line, guard in lines[-1]:
        relay(line, guard)
    while chores:
        chore()
    for group in lines:
        for line, guard in group:
            for part in (0, 1):
                arrive(links.index(line, 1 - links.row, 1 - links.col), part, guard)
            arrive(links.index(line, 1 - links.row, links.col), 0, guard)
            arrive(links.index(line, links.row, 1 - links.col), 1, guard)
    for guard, copy in pending:
        if guard is None:
            copy.wait_send()
        else:
            pl.when(guard)(copy.wait_send)
    own.wait()
    for step in range(1, cores):
        inner_copy(core, step).wait_send()


def gather_tiles(tile, count, full_weight, full_cot, layer_input, gain_row, inv_rms):
    rows, width = tile.shape
    tokens = layer_input.shape[0]
    cores = lax.axis_size("mp")
    vmem = pl.BlockSpec(memory_space=pltpu.VMEM)
    anywhere = pl.BlockSpec(memory_space=pl.ANY)
    return pl.pallas_call(
        functools.partial(gather_kernel, count // PLANE),
        out_shape=(
            jax.ShapeDtypeStruct((count, rows, width), tile.dtype),
            jax.ShapeDtypeStruct((tokens, width), jnp.bfloat16),
        ),
        in_specs=[anywhere, anywhere, vmem, vmem, vmem, vmem],
        out_specs=(anywhere, vmem),
        scratch_shapes=[
            pltpu.VMEM(full_weight.shape, full_weight.dtype),
            pltpu.VMEM((tokens, width), jnp.float32),
            pltpu.VMEM((cores, tokens, 128), jnp.float32),
            pltpu.SemaphoreType.DMA,
            pltpu.SemaphoreType.DMA,
            pltpu.SemaphoreType.DMA((count, 2, 4)),
            pltpu.SemaphoreType.DMA((count, 2)),
            pltpu.SemaphoreType.DMA((cores - 1,)),
            pltpu.SemaphoreType.DMA((cores,)),
        ],
        compiler_params=pltpu.CompilerParams(
            collective_id=1, has_side_effects=True, vmem_limit_bytes=48 * 1024 * 1024
        ),
        cost_estimate=pl.CostEstimate(
            flops=2 * tokens * width * full_weight.shape[0],
            bytes_accessed=6 * count * rows * width,
            transcendentals=0,
        ),
    )(tile, full_weight, full_cot, layer_input, gain_row, inv_rms)


def scatter_kernel(
    planes,
    clipped_ref,
    normed_ref,
    seed_ref,
    out_ref,
    part_ref,
    total_ref,
    first_in,
    second_in,
    line_in,
    second_out,
    line_out,
    send_sems,
    first_sems,
    second_sems,
    line_sems,
):
    links = Links(planes)
    rows, width = out_ref.shape
    half = width // 2
    block = 16
    links.greet()
    pending = []
    row, col, place = links.row, links.col, links.line
    order = sorted(range(planes), key=lambda line: -max(line, planes - 1 - line))
    first_peer = (links.row_peer(), links.col_peer())
    second_peer = (links.col_peer(), links.row_peer())

    def columns(part):
        return pl.ds(part * half, half)

    def first_copy(line, part):
        if part == 0:
            source = part_ref.at[line, 1 - row, :, :, columns(0)]
        else:
            source = part_ref.at[line, :, 1 - col, :, columns(1)]
        return remote(
            source,
            first_in.at[line, part],
            send_sems.at[line, part, 0],
            first_sems.at[line, part],
            first_peer[part],
        )

    def second_copy(line, part):
        return remote(
            second_out.at[line, part],
            second_in.at[line, part],
            send_sems.at[line, part, 1],
            second_sems.at[line, part],
            second_peer[part],
        )

    def line_copy(line, part, side):
        return remote(
            line_out.at[line, part],
            line_in.at[side, line, part],
            send_sems.at[line, part, 2],
            line_sems.at[side, line, part],
            links.above() if side == 0 else links.below(),
        )

    def make_tiles(line):
        plane_rows = PLANE * rows
        tile = width // 8

        def at(index, carry):
            span = pl.ds(pl.multiple_of(index * tile, tile), tile)
            product = lax.dot_general(
                clipped_ref[:, line * plane_rows : (line + 1) * plane_rows],
                normed_ref[:, span],
                (((0,), (0,)), ((), ())),
                preferred_element_type=jnp.float32,
            )
            for lane in range(PLANE):
                part_ref[line, lane // 2, lane % 2, :, span] = product[
                    lane * rows : (lane + 1) * rows
                ].astype(jnp.bfloat16)
            return carry

        lax.fori_loop(0, 8, at, 0)

    def draw_noise():
        seed = seed_ref[0]
        tile = width // 8
        full_width = width * links.cores
        deep = 8

        def at(index, carry):
            top = pl.multiple_of((index // 8) * deep, deep)
            left = pl.multiple_of((index % 8) * tile, tile)
            row_pos = top + lax.broadcasted_iota(jnp.int32, (deep, tile), 0)
            col_pos = (
                links.mp * width + left + lax.broadcasted_iota(jnp.int32, (deep, tile), 1)
            )
            noise = gauss_noise(seed, row_pos * full_width + col_pos)
            total_ref[pl.ds(top, deep), pl.ds(left, tile)] = NOISE_MULT * CLIP_NORM * noise
            return carry

        lax.fori_loop(0, (rows // deep) * 8, at, 0)

    def send_first(line):
        for part in (0, 1):
            copy = first_copy(line, part)
            copy.start()
            pending.append((None, copy))

    def by_blocks(step):
        def at(index, carry):
            step(pl.ds(pl.multiple_of(index * block, block), block))
            return carry

        lax.fori_loop(0, rows // block, at, 0)

    def send_second(line):
        for part in (0, 1):
            first_copy(line, part).wait_recv()
            give_row, give_col = (row, 1 - col) if part == 0 else (1 - row, col)
            lane = 1 - col if part == 0 else 1 - row

            def step(at):
                second_out[line, part, at, :] = (
                    part_ref[line, give_row, give_col, at, columns(part)].astype(jnp.float32)
                    + first_in[line, part, lane, at, :].astype(jnp.float32)
                ).astype(jnp.bfloat16)

            by_blocks(step)
            copy = second_copy(line, part)
            copy.start()
            pending.append((None, copy))

    def plane_sum(line, part, at):
        lane = col if part == 0 else row
        return (
            part_ref[line, row, col, at, columns(part)].astype(jnp.float32)
            + first_in[line, part, lane, at, :].astype(jnp.float32)
            + second_in[line, part, at, :].astype(jnp.float32)
        )

    def send_line(line):
        for part in (0, 1):
            second_copy(line, part).wait_recv()

            @pl.when(place == line)
            def _():
                def step(at):
                    total_ref[at, columns(part)] += plane_sum(line, part, at)

                by_blocks(step)

            for side, sends, joins in (
                (0, place < line, place > 0),
                (1, place > line, place < planes - 1),
            ):

                @pl.when(jnp.logical_and(sends, joins))
                def _():
                    line_copy(line, part, side).wait_recv()

                    def step(at):
                        line_out[line, part, at, :] = (
                            plane_sum(line, part, at)
                            + line_in[side, line, part, at, :].astype(jnp.float32)
                        ).astype(jnp.bfloat16)

                    by_blocks(step)

                @pl.when(jnp.logical_and(sends, jnp.logical_not(joins)))
                def _():
                    def step(at):
                        line_out[line, part, at, :] = plane_sum(line, part, at).astype(jnp.bfloat16)

                    by_blocks(step)

                copy = line_copy(line, part, side)
                pl.when(sends)(copy.start)
                pending.append((sends, copy))

    ahead = 2
    for line in order[:ahead]:
        make_tiles(line)
        send_first(line)
    draw_noise()
    for index, line in enumerate(order):
        send_second(line)
        if index + ahead < planes:
            make_tiles(order[index + ahead])
            send_first(order[index + ahead])
        if index > 0:
            send_line(order[index - 1])
    send_line(order[-1])

    for side, joins in ((0, place > 0), (1, place < planes - 1)):
        for part in (0, 1):

            @pl.when(joins)
            def _():
                line_copy(place, part, side).wait_recv()

                def step(at):
                    total_ref[at, columns(part)] += line_in[side, place, part, at, :].astype(
                        jnp.float32
                    )

                by_blocks(step)

    def finish(at):
        out_ref[at, :] = total_ref[at, :].astype(jnp.bfloat16)

    by_blocks(finish)
    for guard, copy in pending:
        if guard is None:
            copy.wait_send()
        else:
            pl.when(guard)(copy.wait_send)


def scatter_sum(clipped, normed, seed, count):
    planes = count // PLANE
    rows = clipped.shape[1] // count
    width = normed.shape[1]
    vmem = pl.BlockSpec(memory_space=pltpu.VMEM)
    half = width // 2
    return pl.pallas_call(
        functools.partial(scatter_kernel, planes),
        out_shape=jax.ShapeDtypeStruct((rows, width), jnp.bfloat16),
        in_specs=[vmem, vmem, pl.BlockSpec(memory_space=pltpu.SMEM)],
        out_specs=vmem,
        scratch_shapes=[
            pltpu.VMEM((planes, 2, 2, rows, width), jnp.bfloat16),
            pltpu.VMEM((rows, width), jnp.float32),
            pltpu.VMEM((planes, 2, 2, rows, half), jnp.bfloat16),
            pltpu.VMEM((planes, 2, rows, half), jnp.bfloat16),
            pltpu.VMEM((2, planes, 2, rows, half), jnp.bfloat16),
            pltpu.VMEM((planes, 2, rows, half), jnp.bfloat16),
            pltpu.VMEM((planes, 2, rows, half), jnp.bfloat16),
            pltpu.SemaphoreType.DMA((planes, 2, 3)),
            pltpu.SemaphoreType.DMA((planes, 2)),
            pltpu.SemaphoreType.DMA((planes, 2)),
            pltpu.SemaphoreType.DMA((2, planes, 2)),
        ],
        compiler_params=pltpu.CompilerParams(
            collective_id=2, has_side_effects=True, vmem_limit_bytes=40 * 1024 * 1024
        ),
        cost_estimate=pl.CostEstimate(
            flops=2 * count * rows * width * clipped.shape[0],
            bytes_accessed=8 * count * rows * width,
            transcendentals=0,
        ),
    )(clipped, normed, seed)


def body(
    layer_input,
    norm_gain,
    value_weight,
    value_cotangent,
    doc_ids,
    owners,
    noise_seeds,
    master,
    moment_one,
    moment_two,
):
    part_width = layer_input.shape[1]
    full_width = part_width * lax.axis_size("mp")
    group_rows = value_weight.shape[0]
    slot_count = master.shape[0] // group_rows
    cycle_size = lax.axis_size("dp")
    my_group = lax.axis_index("dp")
    inputs = layer_input.astype(jnp.float32)
    gain_row = norm_gain.astype(jnp.float32)
    squares = lax.psum(jnp.sum(inputs * inputs, axis=1), "mp")
    inv_rms = lax.rsqrt(squares / full_width + EPS_NORM)[:, None]
    normed = (inputs * inv_rms * gain_row).astype(jnp.bfloat16)
    seed_value = noise_seeds[my_group]
    full_weight = lax.all_gather(value_weight, "dp", axis=0, tiled=True)
    full_cot, clipped = clip_by_document(normed, value_cotangent, doc_ids)
    group_ids = jnp.arange(cycle_size, dtype=jnp.int32)
    earlier = group_ids[:, None] > group_ids[None, :]
    same_owner = owners[:, None] == owners[None, :]
    slot_rank = jnp.sum((earlier & same_owner).astype(jnp.int32), axis=1)
    slot_ids = jnp.arange(slot_count, dtype=jnp.int32)
    holds_slot = (owners[None, :] == my_group) & (slot_rank[None, :] == slot_ids[:, None])
    sources = jnp.sum(jnp.where(holds_slot, group_ids[None, :], 0), axis=1)
    filled = jnp.any(holds_slot, axis=1)
    filled_rows = jnp.repeat(filled, group_rows)
    noisy_tile = scatter_sum(clipped, normed, seed_value[None], cycle_size)
    arrived, input_grad = gather_tiles(
        noisy_tile, cycle_size, full_weight, full_cot, layer_input, gain_row[None, :], inv_rms
    )
    gathered = jnp.take(arrived, sources, axis=0).reshape(slot_count * group_rows, part_width)
    gathered = gathered.astype(jnp.float32)
    first_new = BETA_ONE * moment_one + (1.0 - BETA_ONE) * gathered
    second_new = BETA_TWO * moment_two + (1.0 - BETA_TWO) * gathered * gathered
    update = (
        first_new
        / (1.0 - BETA_ONE**ADAM_STEP)
        / (jnp.sqrt(second_new / (1.0 - BETA_TWO**ADAM_STEP)) + ADAM_EPS)
    )
    master_new = master - LEARN_RATE * update
    keep_mask = filled_rows[:, None]
    new_master = jnp.where(keep_mask, master_new, master)
    new_moment_one = jnp.where(keep_mask, first_new, moment_one)
    new_moment_two = jnp.where(keep_mask, second_new, moment_two)
    return (input_grad, new_master, new_moment_one, new_moment_two)


def solution(mesh):
    in_specs = (
        P("dp", "mp"),
        P("mp"),
        P("dp", "mp"),
        P("dp", "mp"),
        P("dp"),
        P(),
        P(),
        P("dp", "mp"),
        P("dp", "mp"),
        P("dp", "mp"),
    )
    out_specs = (P("dp", "mp"), P("dp", "mp"), P("dp", "mp"), P("dp", "mp"))
    return jax.shard_map(body, mesh=mesh, in_specs=in_specs, out_specs=out_specs, check_vma=False)
```

```python
import functools

import jax
import jax.numpy as jnp
from jax import lax
from jax.experimental import pallas as pl
from jax.experimental.pallas import tpu as pltpu
from jax.sharding import PartitionSpec as P

EPS_NORM = 1e-06
CLIP_NORM = 128.0
NOISE_MULT = 0.01
LEARN_RATE = 0.001
BETA_ONE = 0.9
BETA_TWO = 0.999
ADAM_STEP = 100
ADAM_EPS = 1e-08


def mix_bits(bits_in):
    bits_in = jnp.bitwise_xor(bits_in, lax.shift_right_logical(bits_in, jnp.int32(16)))
    bits_in = bits_in * jnp.int32(2146121005)
    bits_in = jnp.bitwise_xor(bits_in, lax.shift_right_logical(bits_in, jnp.int32(15)))
    bits_in = bits_in * jnp.int32(-2073254261)
    bits_in = jnp.bitwise_xor(bits_in, lax.shift_right_logical(bits_in, jnp.int32(16)))
    return bits_in


def unit_draw(seed_value, position):
    hashed = mix_bits(mix_bits(jnp.bitwise_xor(position, seed_value)) + seed_value)
    return (lax.shift_right_logical(hashed, jnp.int32(8)).astype(jnp.float32) + 0.5) * (
        1.0 / 16777216.0
    )


def gauss_noise(seed_value, position):
    draw_one = unit_draw(seed_value, 2 * position)
    draw_two = unit_draw(seed_value, 2 * position + 1)
    return jnp.sqrt(-2.0 * jnp.log(draw_one)) * jnp.cos(6.283185307179586 * draw_two)


PLANE = 4


class Links:
    def __init__(self, planes):
        self.planes = planes
        me = lax.axis_index("dp")
        self.mp = lax.axis_index("mp")
        self.me = me
        self.cores = lax.axis_size("mp")
        self.line = me // PLANE
        self.row = (me // 2) % 2
        self.col = me % 2

    def index(self, line, row, col):
        return line * PLANE + row * 2 + col

    def col_peer(self):
        return (self.index(self.line, self.row, 1 - self.col), self.mp)

    def row_peer(self):
        return (self.index(self.line, 1 - self.row, self.col), self.mp)

    def above(self):
        return (self.index(self.line + 1, self.row, self.col), self.mp)

    def below(self):
        return (self.index(self.line - 1, self.row, self.col), self.mp)

    def has_above(self):
        return self.line + 1 < self.planes

    def has_below(self):
        return self.line > 0

    def core_peer(self, step):
        return (self.me, (self.mp + step) % self.cores)

    def greet(self, with_cores=False):
        barrier = pltpu.get_barrier_semaphore()
        mesh_ids = pl.DeviceIdType.MESH
        for peer in (self.col_peer(), self.row_peer()):
            pl.semaphore_signal(barrier, inc=1, device_id=peer, device_id_type=mesh_ids)

        @pl.when(self.has_above())
        def _():
            pl.semaphore_signal(barrier, inc=1, device_id=self.above(), device_id_type=mesh_ids)

        @pl.when(self.has_below())
        def _():
            pl.semaphore_signal(barrier, inc=1, device_id=self.below(), device_id_type=mesh_ids)

        ends = jnp.where(self.line > 0, 1, 0) + jnp.where(self.line + 1 < self.planes, 1, 0)
        others = 0
        if with_cores:
            others = self.cores - 1
            for step in range(1, self.cores):
                pl.semaphore_signal(
                    barrier, inc=1, device_id=self.core_peer(step), device_id_type=mesh_ids
                )
        pl.semaphore_wait(barrier, 2 + others + ends)


def remote(src, dst, send_sem, recv_sem, peer):
    return pltpu.make_async_remote_copy(
        src_ref=src,
        dst_ref=dst,
        send_sem=send_sem,
        recv_sem=recv_sem,
        device_id=peer,
        device_id_type=pl.DeviceIdType.MESH,
    )


def run_gather(links, planes, tile_ref, out_ref, own_sem, send_sems, recv_sems, chores):
    width = tile_ref.shape[1]
    extra = 2 * ((width // 128) * 3 // 32) * 128
    half = (width - extra) // 2
    spans = (pl.ds(0, half), pl.ds(half, half), pl.ds(2 * half, extra))
    line, row, col = links.line, links.row, links.col
    mine = links.index(line, row, col)
    ways = (links.col_peer(), links.row_peer(), links.above(), links.below())
    pending = []

    def transfer(shard, part, way, from_tile=False):
        target = out_ref.at[shard, :, spans[part]]
        return remote(
            tile_ref.at[:, spans[part]] if from_tile else target,
            target,
            send_sems.at[shard, part, way],
            recv_sems.at[shard, part],
            ways[way],
        )

    def start(shard, part, way, guard, from_tile=False):
        copy = transfer(shard, part, way, from_tile)
        pending.append((guard, copy))
        if guard is None:
            copy.start()
        else:
            pl.when(guard)(copy.start)

    def arrive(shard, part, guard):
        copy = transfer(shard, part, 0)
        if guard is None:
            copy.wait_recv()
        else:
            pl.when(guard)(copy.wait_recv)

    def both(first, second):
        return jnp.logical_and(first, second)

    def chore():
        if chores:
            chores.pop(0)()

    def spread(at, guard, from_tile):
        shard = links.index(at, row, col)
        start(shard, 0, 0, guard, from_tile)
        start(shard, 1, 1, guard, from_tile)
        start(shard, 0, 1, guard, from_tile)
        start(shard, 1, 0, guard, from_tile)

    def relay(at, guard):
        shard = links.index(at, row, 1 - col)
        arrive(shard, 0, guard)
        start(shard, 0, 1, guard)
        shard = links.index(at, 1 - row, col)
        arrive(shard, 1, guard)
        start(shard, 1, 0, guard)

    def leave_plane():
        for far_col in (col, 1 - col):
            arrive(links.index(line, 1 - row, far_col), 2, None)
        for at_row in (row, 1 - row):
            for at_col in (col, 1 - col):
                own = at_row is row and at_col is col
                shard = links.index(line, at_row, at_col)
                start(shard, 2, 2, links.has_above(), own)
                start(shard, 2, 3, links.has_below(), own)

    def carry(step):
        for at, guard, way, onward in (
            (line - step, line - step >= 0, 2, links.has_above()),
            (line + step, line + step < planes, 3, links.has_below()),
        ):
            for lane in range(PLANE):
                shard = at * PLANE + lane
                arrive(shard, 2, guard)
                start(shard, 2, way, both(guard, onward))

    own = pltpu.make_async_copy(tile_ref, out_ref.at[mine], own_sem)
    own.start()
    for part in (0, 1):
        start(mine, part, 2, links.has_above(), True)
        start(mine, part, 3, links.has_below(), True)
    if extra:
        start(mine, 2, 0, None, True)
        start(mine, 2, 1, None, True)
    spread(line, None, True)
    chore()
    if extra:
        shard = links.index(line, row, 1 - col)
        arrive(shard, 2, None)
        start(shard, 2, 1, None)
    lines = [[(line, None)]]
    carried = 0
    for step in range(1, planes):
        below, above = line - step, line + step
        got_below, got_above = below >= 0, above < planes
        for part in (0, 1):
            shard = links.index(below, row, col)
            arrive(shard, part, got_below)
            start(shard, part, 2, both(got_below, links.has_above()))
            shard = links.index(above, row, col)
            arrive(shard, part, got_above)
            start(shard, part, 3, both(got_above, links.has_below()))
        spread(below, got_below, False)
        spread(above, got_above, False)
        if extra and step == min(2, planes - 1):
            leave_plane()
        if extra and step > 2:
            carried += 1
            carry(carried)
        for at, guard in lines[-1]:
            relay(at, guard)
        chore()
        lines.append([(below, got_below), (above, got_above)])
    if extra and carried < planes - 1:
        carried += 1
        carry(carried)
    for at, guard in lines[-1]:
        relay(at, guard)
    while chores:
        chore()
    if extra:
        for step in range(carried + 1, planes):
            carry(step)
    for group in lines:
        for at, guard in group:
            for part in (0, 1):
                arrive(links.index(at, 1 - row, 1 - col), part, guard)
            arrive(links.index(at, 1 - row, col), 0, guard)
            arrive(links.index(at, row, 1 - col), 1, guard)
    for guard, copy in pending:
        if guard is None:
            copy.wait_send()
        else:
            pl.when(guard)(copy.wait_send)
    own.wait()


def gather_scratch(count):
    return [
        pltpu.SemaphoreType.DMA,
        pltpu.SemaphoreType.DMA((count, 3, 4)),
        pltpu.SemaphoreType.DMA((count, 3)),
    ]


def by_columns(width, step):
    tile = width // 8

    def at(index, carry):
        step(pl.ds(pl.multiple_of(index * tile, tile), tile))
        return carry

    lax.fori_loop(0, 8, at, 0)


def lane_sums(values):
    total = values[:, :128]
    for lane in range(1, values.shape[1] // 128):
        total = total + values[:, lane * 128 : (lane + 1) * 128]
    return total


def clip_kernel(
    planes,
    tile_ref,
    input_hbm,
    gain_ref,
    cot_ref,
    doc_col_ref,
    doc_row_ref,
    weight_ref,
    full_ref,
    clipped_ref,
    normed_ref,
    inv_ref,
    input_ref,
    squares,
    grams,
    own_sem,
    gather_send,
    gather_recv,
    input_sem,
    send_sems,
    recv_sems,
):
    links = Links(planes)
    me, cores = links.mp, links.cores
    tokens, cot_width = cot_ref.shape
    width = input_ref.shape[1]
    block = tokens // 2
    steps = range(1, cores)
    fetch = pltpu.make_async_copy(input_hbm, input_ref, input_sem)
    fetch.start()
    links.greet(True)

    def cot_slot(core):
        return full_ref.at[:, pl.ds(pl.multiple_of(core * cot_width, cot_width), cot_width)]

    def cot_copy(core, step):
        return remote(
            cot_ref,
            cot_slot(core),
            send_sems.at[step - 1, 0],
            recv_sems.at[core, 0],
            links.core_peer(step),
        )

    def gram_copy(core, step, part):
        rows = pl.ds(part * block, block)
        return remote(
            grams.at[core, rows],
            grams.at[core, rows],
            send_sems.at[step - 1, 1 + part],
            recv_sems.at[core, 1 + part],
            links.core_peer(step),
        )

    def square_copy(core, step):
        return remote(
            squares.at[core],
            squares.at[core],
            send_sems.at[step - 1, 3],
            recv_sems.at[core, 3],
            links.core_peer(step),
        )

    def norm_and_grams():
        for step in steps:
            cot_copy(me, step).start()
        fetch.wait()
        squares[me] = jnp.zeros(squares.shape[1:], jnp.float32)

        def square(columns):
            values = input_ref[:, columns].astype(jnp.float32)
            squares[me] = squares[me] + lane_sums(values * values)

        by_columns(width, square)
        for step in steps:
            square_copy(me, step).start()
        full_ref[:, pl.ds(pl.multiple_of(me * cot_width, cot_width), cot_width)] = cot_ref[...]
        for step in steps:
            square_copy((me + step) % cores, step).wait_recv()
        total = squares[0]
        for core in range(1, cores):
            total = total + squares[core]
        mean = jnp.sum(total, axis=1, keepdims=True) / (width * cores)
        inv = lax.rsqrt(mean + EPS_NORM)
        inv_ref[...] = inv

        def norm(columns):
            values = input_ref[:, columns].astype(jnp.float32)
            normed_ref[:, columns] = (values * inv * gain_ref[:, columns]).astype(jnp.bfloat16)

        by_columns(width, norm)
        for part in range(2):
            grams[me, pl.ds(part * block, block), :] = lax.dot_general(
                normed_ref[pl.ds(part * block, block), :],
                normed_ref[...],
                (((1,), (1,)), ((), ())),
                preferred_element_type=jnp.float32,
            )
            for step in steps:
                gram_copy(me, step, part).start()

    def clip():
        for step in steps:
            cot_copy((me + step) % cores, step).wait_recv()
        gram_values = lax.dot_general(
            full_ref[...],
            full_ref[...],
            (((1,), (1,)), ((), ())),
            preferred_element_type=jnp.float32,
        )
        same_doc = doc_col_ref[...] == doc_row_ref[...]
        for step in steps:
            for part in range(2):
                gram_copy((me + step) % cores, step, part).wait_recv()
        gram_features = grams[0]
        for core in range(1, cores):
            gram_features = gram_features + grams[core]
        product = jnp.where(same_doc, gram_features * gram_values, 0.0)
        row_sums = jnp.sum(product, axis=0, keepdims=True)
        squared = jnp.sum(jnp.where(same_doc, row_sums, 0.0), axis=1, keepdims=True)
        scales = CLIP_NORM / (jnp.sqrt(squared) + 0.01)
        clipped_ref[...] = (full_ref[...].astype(jnp.float32) * scales).astype(jnp.bfloat16)
        for step in steps:
            cot_copy(me, step).wait_send()
            square_copy(me, step).wait_send()
            for part in range(2):
                gram_copy(me, step, part).wait_send()

    run_gather(
        links,
        planes,
        tile_ref,
        weight_ref,
        own_sem,
        gather_send,
        gather_recv,
        [norm_and_grams, clip],
    )


def gather_and_clip(weight, layer_input, gain_row, cot, doc_ids, count):
    tokens, cot_width = cot.shape
    rows, width = weight.shape
    cores = lax.axis_size("mp")
    vmem = pl.BlockSpec(memory_space=pltpu.VMEM)
    anywhere = pl.BlockSpec(memory_space=pl.ANY)
    full = jax.ShapeDtypeStruct((tokens, cot_width * cores), cot.dtype)
    return pl.pallas_call(
        functools.partial(clip_kernel, count // PLANE),
        out_shape=(
            jax.ShapeDtypeStruct((count, rows, width), weight.dtype),
            full,
            full,
            jax.ShapeDtypeStruct((tokens, width), jnp.bfloat16),
            jax.ShapeDtypeStruct((tokens, 1), jnp.float32),
        ),
        in_specs=[anywhere, anywhere, vmem, vmem, vmem, vmem],
        out_specs=(anywhere, vmem, vmem, vmem, vmem),
        scratch_shapes=[
            pltpu.VMEM((tokens, width), jnp.bfloat16),
            pltpu.VMEM((cores, tokens, 128), jnp.float32),
            pltpu.VMEM((cores, tokens, tokens), jnp.float32),
            *gather_scratch(count),
            pltpu.SemaphoreType.DMA,
            pltpu.SemaphoreType.DMA((cores - 1, 4)),
            pltpu.SemaphoreType.DMA((cores, 4)),
        ],
        compiler_params=pltpu.CompilerParams(
            collective_id=3, has_side_effects=True, vmem_limit_bytes=40 * 1024 * 1024
        ),
        cost_estimate=pl.CostEstimate(
            flops=2 * tokens * tokens * (width + cot_width * cores),
            bytes_accessed=4 * tokens * width + 4 * count * rows * width,
            transcendentals=0,
        ),
    )(weight, layer_input, gain_row, cot, doc_ids[:, None], doc_ids[None, :])


def gather_kernel(
    planes,
    tile_ref,
    weight_hbm,
    cot_ref,
    input_ref,
    gain_ref,
    inv_ref,
    out_ref,
    grad_ref,
    weight_ref,
    weighted_ref,
    inner_ref,
    own_sem,
    send_sems,
    recv_sems,
    weight_sem,
    inner_send,
    inner_recv,
):
    links = Links(planes)
    core, cores = links.mp, links.cores
    width = input_ref.shape[1]
    tile = width // 8
    fetch = pltpu.make_async_copy(weight_hbm, weight_ref, weight_sem)
    fetch.start()
    links.greet(True)

    def inner_copy(slot, step):
        return remote(
            inner_ref.at[slot],
            inner_ref.at[slot],
            inner_send.at[step - 1],
            inner_recv.at[slot],
            links.core_peer(step),
        )

    def project(low, high):
        def at(index, carry):
            columns = pl.ds(pl.multiple_of(index * tile, tile), tile)
            weighted = gain_ref[:, columns] * jnp.dot(
                cot_ref[...], weight_ref[:, columns], preferred_element_type=jnp.float32
            )
            weighted_ref[:, columns] = weighted
            product = weighted * input_ref[:, columns].astype(jnp.float32)
            total = inner_ref[core]
            for lane in range(tile // 128):
                total = total + product[:, lane * 128 : (lane + 1) * 128]
            inner_ref[core] = total
            return carry

        lax.fori_loop(low, high, at, 0)

    def project_first():
        inner_ref[core] = jnp.zeros(inner_ref.shape[1:], jnp.float32)
        fetch.wait()
        project(0, 4)

    def project_rest():
        project(4, 8)
        for step in range(1, cores):
            inner_copy(core, step).start()

    def inner_done():
        for step in range(1, cores):
            inner_copy((core + step) % cores, step).wait_recv()
        total = inner_ref[0]
        for slot in range(1, cores):
            total = total + inner_ref[slot]
        inner = jnp.sum(total, axis=1, keepdims=True) / (width * cores)
        inv = inv_ref[...]
        factor = inv * inv * inv * inner

        def at(index, carry):
            columns = pl.ds(pl.multiple_of(index * tile, tile), tile)
            grad_ref[:, columns] = (
                inv * weighted_ref[:, columns] - input_ref[:, columns].astype(jnp.float32) * factor
            ).astype(jnp.bfloat16)
            return carry

        lax.fori_loop(0, 8, at, 0)

    run_gather(
        links,
        planes,
        tile_ref,
        out_ref,
        own_sem,
        send_sems,
        recv_sems,
        [project_first, project_rest, inner_done],
    )
    for step in range(1, cores):
        inner_copy(core, step).wait_send()


def gather_tiles(tile, count, full_weight, full_cot, layer_input, gain_row, inv_rms):
    rows, width = tile.shape
    tokens = layer_input.shape[0]
    cores = lax.axis_size("mp")
    vmem = pl.BlockSpec(memory_space=pltpu.VMEM)
    anywhere = pl.BlockSpec(memory_space=pl.ANY)
    return pl.pallas_call(
        functools.partial(gather_kernel, count // PLANE),
        out_shape=(
            jax.ShapeDtypeStruct((count, rows, width), tile.dtype),
            jax.ShapeDtypeStruct((tokens, width), jnp.bfloat16),
        ),
        in_specs=[anywhere, anywhere, vmem, vmem, vmem, vmem],
        out_specs=(anywhere, vmem),
        scratch_shapes=[
            pltpu.VMEM(full_weight.shape, full_weight.dtype),
            pltpu.VMEM((tokens, width), jnp.float32),
            pltpu.VMEM((cores, tokens, 128), jnp.float32),
            *gather_scratch(count),
            pltpu.SemaphoreType.DMA,
            pltpu.SemaphoreType.DMA((cores - 1,)),
            pltpu.SemaphoreType.DMA((cores,)),
        ],
        compiler_params=pltpu.CompilerParams(
            collective_id=1, has_side_effects=True, vmem_limit_bytes=48 * 1024 * 1024
        ),
        cost_estimate=pl.CostEstimate(
            flops=2 * tokens * width * full_weight.shape[0],
            bytes_accessed=6 * count * rows * width,
            transcendentals=0,
        ),
    )(tile, full_weight, full_cot, layer_input, gain_row, inv_rms)


def scatter_kernel(
    planes,
    clipped_ref,
    normed_ref,
    seed_ref,
    out_ref,
    part_ref,
    total_ref,
    first_in,
    second_in,
    line_in,
    second_out,
    line_out,
    send_sems,
    first_sems,
    second_sems,
    line_sems,
):
    links = Links(planes)
    rows, width = out_ref.shape
    half = width // 2
    block = 16
    links.greet()
    pending = []
    row, col, place = links.row, links.col, links.line
    order = sorted(range(planes), key=lambda line: -max(line, planes - 1 - line))
    first_peer = (links.row_peer(), links.col_peer())
    second_peer = (links.col_peer(), links.row_peer())

    def columns(part):
        return pl.ds(part * half, half)

    def first_copy(line, part):
        if part == 0:
            source = part_ref.at[line, 1 - row, :, :, columns(0)]
        else:
            source = part_ref.at[line, :, 1 - col, :, columns(1)]
        return remote(
            source,
            first_in.at[line, part],
            send_sems.at[line, part, 0],
            first_sems.at[line, part],
            first_peer[part],
        )

    def second_copy(line, part):
        return remote(
            second_out.at[line, part],
            second_in.at[line, part],
            send_sems.at[line, part, 1],
            second_sems.at[line, part],
            second_peer[part],
        )

    def line_copy(line, part, side):
        return remote(
            line_out.at[line, part],
            line_in.at[side, line, part],
            send_sems.at[line, part, 2],
            line_sems.at[side, line, part],
            links.above() if side == 0 else links.below(),
        )

    def make_tiles(line):
        plane_rows = PLANE * rows
        tile = width // 8

        def at(index, carry):
            span = pl.ds(pl.multiple_of(index * tile, tile), tile)
            product = lax.dot_general(
                clipped_ref[:, line * plane_rows : (line + 1) * plane_rows],
                normed_ref[:, span],
                (((0,), (0,)), ((), ())),
                preferred_element_type=jnp.float32,
            )
            for lane in range(PLANE):
                part_ref[line, lane // 2, lane % 2, :, span] = product[
                    lane * rows : (lane + 1) * rows
                ].astype(jnp.bfloat16)
            return carry

        lax.fori_loop(0, 8, at, 0)

    def draw_noise():
        seed = seed_ref[0]
        tile = width // 8
        full_width = width * links.cores
        deep = 8

        def at(index, carry):
            top = pl.multiple_of((index // 8) * deep, deep)
            left = pl.multiple_of((index % 8) * tile, tile)
            row_pos = top + lax.broadcasted_iota(jnp.int32, (deep, tile), 0)
            col_pos = (
                links.mp * width + left + lax.broadcasted_iota(jnp.int32, (deep, tile), 1)
            )
            noise = gauss_noise(seed, row_pos * full_width + col_pos)
            total_ref[pl.ds(top, deep), pl.ds(left, tile)] = NOISE_MULT * CLIP_NORM * noise
            return carry

        lax.fori_loop(0, (rows // deep) * 8, at, 0)

    def send_first(line):
        for part in (0, 1):
            copy = first_copy(line, part)
            copy.start()
            pending.append((None, copy))

    def by_blocks(step):
        def at(index, carry):
            step(pl.ds(pl.multiple_of(index * block, block), block))
            return carry

        lax.fori_loop(0, rows // block, at, 0)

    def send_second(line):
        for part in (0, 1):
            first_copy(line, part).wait_recv()
            give_row, give_col = (row, 1 - col) if part == 0 else (1 - row, col)
            lane = 1 - col if part == 0 else 1 - row

            def step(at):
                second_out[line, part, at, :] = (
                    part_ref[line, give_row, give_col, at, columns(part)].astype(jnp.float32)
                    + first_in[line, part, lane, at, :].astype(jnp.float32)
                ).astype(jnp.bfloat16)

            by_blocks(step)
            copy = second_copy(line, part)
            copy.start()
            pending.append((None, copy))

    def plane_sum(line, part, at):
        lane = col if part == 0 else row
        return (
            part_ref[line, row, col, at, columns(part)].astype(jnp.float32)
            + first_in[line, part, lane, at, :].astype(jnp.float32)
            + second_in[line, part, at, :].astype(jnp.float32)
        )

    def send_line(line):
        for part in (0, 1):
            second_copy(line, part).wait_recv()

            @pl.when(place == line)
            def _():
                def step(at):
                    total_ref[at, columns(part)] += plane_sum(line, part, at)

                by_blocks(step)

            for side, sends, joins in (
                (0, place < line, place > 0),
                (1, place > line, place < planes - 1),
            ):

                @pl.when(jnp.logical_and(sends, joins))
                def _():
                    line_copy(line, part, side).wait_recv()

                    def step(at):
                        line_out[line, part, at, :] = (
                            plane_sum(line, part, at)
                            + line_in[side, line, part, at, :].astype(jnp.float32)
                        ).astype(jnp.bfloat16)

                    by_blocks(step)

                @pl.when(jnp.logical_and(sends, jnp.logical_not(joins)))
                def _():
                    def step(at):
                        line_out[line, part, at, :] = plane_sum(line, part, at).astype(jnp.bfloat16)

                    by_blocks(step)

                copy = line_copy(line, part, side)
                pl.when(sends)(copy.start)
                pending.append((sends, copy))

    ahead = 2
    for line in order[:ahead]:
        make_tiles(line)
        send_first(line)
    draw_noise()
    for index, line in enumerate(order):
        send_second(line)
        if index + ahead < planes:
            make_tiles(order[index + ahead])
            send_first(order[index + ahead])
        if index > 0:
            send_line(order[index - 1])
    send_line(order[-1])

    for side, joins in ((0, place > 0), (1, place < planes - 1)):
        for part in (0, 1):

            @pl.when(joins)
            def _():
                line_copy(place, part, side).wait_recv()

                def step(at):
                    total_ref[at, columns(part)] += line_in[side, place, part, at, :].astype(
                        jnp.float32
                    )

                by_blocks(step)

    def finish(at):
        out_ref[at, :] = total_ref[at, :].astype(jnp.bfloat16)

    by_blocks(finish)
    for guard, copy in pending:
        if guard is None:
            copy.wait_send()
        else:
            pl.when(guard)(copy.wait_send)


def scatter_sum(clipped, normed, seed, count):
    planes = count // PLANE
    rows = clipped.shape[1] // count
    width = normed.shape[1]
    vmem = pl.BlockSpec(memory_space=pltpu.VMEM)
    half = width // 2
    return pl.pallas_call(
        functools.partial(scatter_kernel, planes),
        out_shape=jax.ShapeDtypeStruct((rows, width), jnp.bfloat16),
        in_specs=[vmem, vmem, pl.BlockSpec(memory_space=pltpu.SMEM)],
        out_specs=vmem,
        scratch_shapes=[
            pltpu.VMEM((planes, 2, 2, rows, width), jnp.bfloat16),
            pltpu.VMEM((rows, width), jnp.float32),
            pltpu.VMEM((planes, 2, 2, rows, half), jnp.bfloat16),
            pltpu.VMEM((planes, 2, rows, half), jnp.bfloat16),
            pltpu.VMEM((2, planes, 2, rows, half), jnp.bfloat16),
            pltpu.VMEM((planes, 2, rows, half), jnp.bfloat16),
            pltpu.VMEM((planes, 2, rows, half), jnp.bfloat16),
            pltpu.SemaphoreType.DMA((planes, 2, 3)),
            pltpu.SemaphoreType.DMA((planes, 2)),
            pltpu.SemaphoreType.DMA((planes, 2)),
            pltpu.SemaphoreType.DMA((2, planes, 2)),
        ],
        compiler_params=pltpu.CompilerParams(
            collective_id=2, has_side_effects=True, vmem_limit_bytes=40 * 1024 * 1024
        ),
        cost_estimate=pl.CostEstimate(
            flops=2 * count * rows * width * clipped.shape[0],
            bytes_accessed=8 * count * rows * width,
            transcendentals=0,
        ),
    )(clipped, normed, seed)


def body(
    layer_input,
    norm_gain,
    value_weight,
    value_cotangent,
    doc_ids,
    owners,
    noise_seeds,
    master,
    moment_one,
    moment_two,
):
    part_width = layer_input.shape[1]
    group_rows = value_weight.shape[0]
    slot_count = master.shape[0] // group_rows
    cycle_size = lax.axis_size("dp")
    my_group = lax.axis_index("dp")
    gain_row = norm_gain.astype(jnp.float32)[None, :]
    seed_value = noise_seeds[my_group]
    full_weight, full_cot, clipped, normed, inv_rms = gather_and_clip(
        value_weight, layer_input, gain_row, value_cotangent, doc_ids, cycle_size
    )
    full_weight = full_weight.reshape(cycle_size * group_rows, part_width)
    group_ids = jnp.arange(cycle_size, dtype=jnp.int32)
    earlier = group_ids[:, None] > group_ids[None, :]
    same_owner = owners[:, None] == owners[None, :]
    slot_rank = jnp.sum((earlier & same_owner).astype(jnp.int32), axis=1)
    slot_ids = jnp.arange(slot_count, dtype=jnp.int32)
    holds_slot = (owners[None, :] == my_group) & (slot_rank[None, :] == slot_ids[:, None])
    sources = jnp.sum(jnp.where(holds_slot, group_ids[None, :], 0), axis=1)
    filled = jnp.any(holds_slot, axis=1)
    filled_rows = jnp.repeat(filled, group_rows)
    noisy_tile = scatter_sum(clipped, normed, seed_value[None], cycle_size)
    arrived, input_grad = gather_tiles(
        noisy_tile, cycle_size, full_weight, full_cot, layer_input, gain_row, inv_rms
    )
    gathered = jnp.take(arrived, sources, axis=0).reshape(slot_count * group_rows, part_width)
    gathered = gathered.astype(jnp.float32)
    first_new = BETA_ONE * moment_one + (1.0 - BETA_ONE) * gathered
    second_new = BETA_TWO * moment_two + (1.0 - BETA_TWO) * gathered * gathered
    update = (
        first_new
        / (1.0 - BETA_ONE**ADAM_STEP)
        / (jnp.sqrt(second_new / (1.0 - BETA_TWO**ADAM_STEP)) + ADAM_EPS)
    )
    master_new = master - LEARN_RATE * update
    keep_mask = filled_rows[:, None]
    new_master = jnp.where(keep_mask, master_new, master)
    new_moment_one = jnp.where(keep_mask, first_new, moment_one)
    new_moment_two = jnp.where(keep_mask, second_new, moment_two)
    return (input_grad, new_master, new_moment_one, new_moment_two)


def solution(mesh):
    in_specs = (
        P("dp", "mp"),
        P("mp"),
        P("dp", "mp"),
        P("dp", "mp"),
        P("dp"),
        P(),
        P(),
        P("dp", "mp"),
        P("dp", "mp"),
        P("dp", "mp"),
    )
    out_specs = (P("dp", "mp"), P("dp", "mp"), P("dp", "mp"), P("dp", "mp"))
    return jax.shard_map(body, mesh=mesh, in_specs=in_specs, out_specs=out_specs, check_vma=False)
```

```python
import functools

import jax
import jax.numpy as jnp
from jax import lax
from jax.experimental import pallas as pl
from jax.experimental.pallas import tpu as pltpu
from jax.sharding import PartitionSpec as P

EPS_NORM = 1e-06
CLIP_NORM = 128.0
NOISE_MULT = 0.01
LEARN_RATE = 0.001
BETA_ONE = 0.9
BETA_TWO = 0.999
ADAM_STEP = 100
ADAM_EPS = 1e-08


def mix_bits(bits_in):
    bits_in = jnp.bitwise_xor(bits_in, lax.shift_right_logical(bits_in, jnp.int32(16)))
    bits_in = bits_in * jnp.int32(2146121005)
    bits_in = jnp.bitwise_xor(bits_in, lax.shift_right_logical(bits_in, jnp.int32(15)))
    bits_in = bits_in * jnp.int32(-2073254261)
    bits_in = jnp.bitwise_xor(bits_in, lax.shift_right_logical(bits_in, jnp.int32(16)))
    return bits_in


def unit_draw(seed_value, position):
    hashed = mix_bits(mix_bits(jnp.bitwise_xor(position, seed_value)) + seed_value)
    return (lax.shift_right_logical(hashed, jnp.int32(8)).astype(jnp.float32) + 0.5) * (
        1.0 / 16777216.0
    )


def gauss_noise(seed_value, position):
    draw_one = unit_draw(seed_value, 2 * position)
    draw_two = unit_draw(seed_value, 2 * position + 1)
    return jnp.sqrt(-2.0 * jnp.log(draw_one)) * jnp.cos(6.283185307179586 * draw_two)


PLANE = 4


class Links:
    def __init__(self, planes):
        self.planes = planes
        me = lax.axis_index("dp")
        self.mp = lax.axis_index("mp")
        self.me = me
        self.cores = lax.axis_size("mp")
        self.line = me // PLANE
        self.row = (me // 2) % 2
        self.col = me % 2

    def index(self, line, row, col):
        return line * PLANE + row * 2 + col

    def col_peer(self):
        return (self.index(self.line, self.row, 1 - self.col), self.mp)

    def row_peer(self):
        return (self.index(self.line, 1 - self.row, self.col), self.mp)

    def above(self):
        return (self.index(self.line + 1, self.row, self.col), self.mp)

    def below(self):
        return (self.index(self.line - 1, self.row, self.col), self.mp)

    def has_above(self):
        return self.line + 1 < self.planes

    def has_below(self):
        return self.line > 0

    def core_peer(self, step):
        return (self.me, (self.mp + step) % self.cores)

    def greet(self, with_cores=False):
        barrier = pltpu.get_barrier_semaphore()
        mesh_ids = pl.DeviceIdType.MESH
        for peer in (self.col_peer(), self.row_peer()):
            pl.semaphore_signal(barrier, inc=1, device_id=peer, device_id_type=mesh_ids)

        @pl.when(self.has_above())
        def _():
            pl.semaphore_signal(barrier, inc=1, device_id=self.above(), device_id_type=mesh_ids)

        @pl.when(self.has_below())
        def _():
            pl.semaphore_signal(barrier, inc=1, device_id=self.below(), device_id_type=mesh_ids)

        ends = jnp.where(self.line > 0, 1, 0) + jnp.where(self.line + 1 < self.planes, 1, 0)
        others = 0
        if with_cores:
            others = self.cores - 1
            for step in range(1, self.cores):
                pl.semaphore_signal(
                    barrier, inc=1, device_id=self.core_peer(step), device_id_type=mesh_ids
                )
        pl.semaphore_wait(barrier, 2 + others + ends)


def remote(src, dst, send_sem, recv_sem, peer):
    return pltpu.make_async_remote_copy(
        src_ref=src,
        dst_ref=dst,
        send_sem=send_sem,
        recv_sem=recv_sem,
        device_id=peer,
        device_id_type=pl.DeviceIdType.MESH,
    )


def column_parts(width):
    extra = 2 * ((width // 128) * 3 // 32) * 128
    return (width - extra) // 2, extra


def run_gather(links, planes, tile_ref, out_ref, own_sem, send_sems, recv_sems, chores):
    half, extra = column_parts(tile_ref.shape[1])
    spans = (pl.ds(0, half), pl.ds(half, half), pl.ds(2 * half, extra))
    line, row, col = links.line, links.row, links.col
    mine = links.index(line, row, col)
    ways = (links.col_peer(), links.row_peer(), links.above(), links.below())
    pending = []

    def transfer(shard, part, way, from_tile=False):
        target = out_ref.at[shard, :, spans[part]]
        return remote(
            tile_ref.at[:, spans[part]] if from_tile else target,
            target,
            send_sems.at[shard, part, way],
            recv_sems.at[shard, part],
            ways[way],
        )

    def start(shard, part, way, guard, from_tile=False):
        copy = transfer(shard, part, way, from_tile)
        pending.append((guard, copy))
        if guard is None:
            copy.start()
        else:
            pl.when(guard)(copy.start)

    def arrive(shard, part, guard):
        copy = transfer(shard, part, 0)
        if guard is None:
            copy.wait_recv()
        else:
            pl.when(guard)(copy.wait_recv)

    def both(first, second):
        return jnp.logical_and(first, second)

    def chore():
        if chores:
            chores.pop(0)()

    def spread(at, guard, from_tile):
        shard = links.index(at, row, col)
        start(shard, 0, 0, guard, from_tile)
        start(shard, 1, 1, guard, from_tile)
        start(shard, 0, 1, guard, from_tile)
        start(shard, 1, 0, guard, from_tile)

    def relay(at, guard):
        shard = links.index(at, row, 1 - col)
        arrive(shard, 0, guard)
        start(shard, 0, 1, guard)
        shard = links.index(at, 1 - row, col)
        arrive(shard, 1, guard)
        start(shard, 1, 0, guard)

    def leave_plane():
        for far_col in (col, 1 - col):
            arrive(links.index(line, 1 - row, far_col), 2, None)
        for at_row in (row, 1 - row):
            for at_col in (col, 1 - col):
                own = at_row is row and at_col is col
                shard = links.index(line, at_row, at_col)
                start(shard, 2, 2, links.has_above(), own)
                start(shard, 2, 3, links.has_below(), own)

    def carry(step):
        for at, guard, way, onward in (
            (line - step, line - step >= 0, 2, links.has_above()),
            (line + step, line + step < planes, 3, links.has_below()),
        ):
            for lane in range(PLANE):
                shard = at * PLANE + lane
                arrive(shard, 2, guard)
                start(shard, 2, way, both(guard, onward))

    own = pltpu.make_async_copy(tile_ref, out_ref.at[mine], own_sem)
    own.start()
    for part in (0, 1):
        start(mine, part, 2, links.has_above(), True)
        start(mine, part, 3, links.has_below(), True)
    if extra:
        start(mine, 2, 0, None, True)
        start(mine, 2, 1, None, True)
    spread(line, None, True)
    chore()
    if extra:
        shard = links.index(line, row, 1 - col)
        arrive(shard, 2, None)
        start(shard, 2, 1, None)
    lines = [[(line, None)]]
    carried = 0
    for step in range(1, planes):
        below, above = line - step, line + step
        got_below, got_above = below >= 0, above < planes
        for part in (0, 1):
            shard = links.index(below, row, col)
            arrive(shard, part, got_below)
            start(shard, part, 2, both(got_below, links.has_above()))
            shard = links.index(above, row, col)
            arrive(shard, part, got_above)
            start(shard, part, 3, both(got_above, links.has_below()))
        spread(below, got_below, False)
        spread(above, got_above, False)
        if extra and step == min(2, planes - 1):
            leave_plane()
        if extra and step > 2:
            carried += 1
            carry(carried)
        for at, guard in lines[-1]:
            relay(at, guard)
        chore()
        lines.append([(below, got_below), (above, got_above)])
    if extra and carried < planes - 1:
        carried += 1
        carry(carried)
    for at, guard in lines[-1]:
        relay(at, guard)
    while chores:
        chore()
    if extra:
        for step in range(carried + 1, planes):
            carry(step)
    for group in lines:
        for at, guard in group:
            for part in (0, 1):
                arrive(links.index(at, 1 - row, 1 - col), part, guard)
            arrive(links.index(at, 1 - row, col), 0, guard)
            arrive(links.index(at, row, 1 - col), 1, guard)
    for guard, copy in pending:
        if guard is None:
            copy.wait_send()
        else:
            pl.when(guard)(copy.wait_send)
    own.wait()


def gather_scratch(count):
    return [
        pltpu.SemaphoreType.DMA,
        pltpu.SemaphoreType.DMA((count, 3, 4)),
        pltpu.SemaphoreType.DMA((count, 3)),
    ]


def by_columns(width, step):
    tile = width // 8

    def at(index, carry):
        step(pl.ds(pl.multiple_of(index * tile, tile), tile))
        return carry

    lax.fori_loop(0, 8, at, 0)


def lane_sums(values):
    total = values[:, :128]
    for lane in range(1, values.shape[1] // 128):
        total = total + values[:, lane * 128 : (lane + 1) * 128]
    return total


def clip_kernel(
    planes,
    tile_ref,
    input_hbm,
    gain_ref,
    cot_ref,
    doc_col_ref,
    doc_row_ref,
    weight_ref,
    full_ref,
    clipped_ref,
    normed_ref,
    inv_ref,
    input_ref,
    squares,
    grams,
    own_sem,
    gather_send,
    gather_recv,
    input_sem,
    send_sems,
    recv_sems,
):
    links = Links(planes)
    me, cores = links.mp, links.cores
    tokens, cot_width = cot_ref.shape
    width = input_ref.shape[1]
    block = tokens // 2
    steps = range(1, cores)
    fetch = pltpu.make_async_copy(input_hbm, input_ref, input_sem)
    fetch.start()
    links.greet(True)

    def cot_slot(core):
        return full_ref.at[:, pl.ds(pl.multiple_of(core * cot_width, cot_width), cot_width)]

    def cot_copy(core, step):
        return remote(
            cot_ref,
            cot_slot(core),
            send_sems.at[step - 1, 0],
            recv_sems.at[core, 0],
            links.core_peer(step),
        )

    def gram_copy(core, step, part):
        rows = pl.ds(part * block, block)
        return remote(
            grams.at[core, rows],
            grams.at[core, rows],
            send_sems.at[step - 1, 1 + part],
            recv_sems.at[core, 1 + part],
            links.core_peer(step),
        )

    def square_copy(core, step):
        return remote(
            squares.at[core],
            squares.at[core],
            send_sems.at[step - 1, 3],
            recv_sems.at[core, 3],
            links.core_peer(step),
        )

    def norm_and_grams():
        for step in steps:
            cot_copy(me, step).start()
        fetch.wait()
        squares[me] = jnp.zeros(squares.shape[1:], jnp.float32)

        def square(columns):
            values = input_ref[:, columns].astype(jnp.float32)
            squares[me] = squares[me] + lane_sums(values * values)

        by_columns(width, square)
        for step in steps:
            square_copy(me, step).start()
        full_ref[:, pl.ds(pl.multiple_of(me * cot_width, cot_width), cot_width)] = cot_ref[...]
        for step in steps:
            square_copy((me + step) % cores, step).wait_recv()
        total = squares[0]
        for core in range(1, cores):
            total = total + squares[core]
        mean = jnp.sum(total, axis=1, keepdims=True) / (width * cores)
        inv = lax.rsqrt(mean + EPS_NORM)
        inv_ref[...] = inv

        def norm(columns):
            values = input_ref[:, columns].astype(jnp.float32)
            normed_ref[:, columns] = (values * inv * gain_ref[:, columns]).astype(jnp.bfloat16)

        by_columns(width, norm)
        for part in range(2):
            grams[me, pl.ds(part * block, block), :] = lax.dot_general(
                normed_ref[pl.ds(part * block, block), :],
                normed_ref[...],
                (((1,), (1,)), ((), ())),
                preferred_element_type=jnp.float32,
            )
            for step in steps:
                gram_copy(me, step, part).start()

    def clip():
        for step in steps:
            cot_copy((me + step) % cores, step).wait_recv()
        gram_values = lax.dot_general(
            full_ref[...],
            full_ref[...],
            (((1,), (1,)), ((), ())),
            preferred_element_type=jnp.float32,
        )
        same_doc = doc_col_ref[...] == doc_row_ref[...]
        for step in steps:
            for part in range(2):
                gram_copy((me + step) % cores, step, part).wait_recv()
        gram_features = grams[0]
        for core in range(1, cores):
            gram_features = gram_features + grams[core]
        product = jnp.where(same_doc, gram_features * gram_values, 0.0)
        row_sums = jnp.sum(product, axis=0, keepdims=True)
        squared = jnp.sum(jnp.where(same_doc, row_sums, 0.0), axis=1, keepdims=True)
        scales = CLIP_NORM / (jnp.sqrt(squared) + 0.01)
        clipped_ref[...] = (full_ref[...].astype(jnp.float32) * scales).astype(jnp.bfloat16)
        for step in steps:
            cot_copy(me, step).wait_send()
            square_copy(me, step).wait_send()
            for part in range(2):
                gram_copy(me, step, part).wait_send()

    run_gather(
        links,
        planes,
        tile_ref,
        weight_ref,
        own_sem,
        gather_send,
        gather_recv,
        [norm_and_grams, clip],
    )


def gather_and_clip(weight, layer_input, gain_row, cot, doc_ids, count):
    tokens, cot_width = cot.shape
    rows, width = weight.shape
    cores = lax.axis_size("mp")
    vmem = pl.BlockSpec(memory_space=pltpu.VMEM)
    anywhere = pl.BlockSpec(memory_space=pl.ANY)
    full = jax.ShapeDtypeStruct((tokens, cot_width * cores), cot.dtype)
    return pl.pallas_call(
        functools.partial(clip_kernel, count // PLANE),
        out_shape=(
            jax.ShapeDtypeStruct((count, rows, width), weight.dtype),
            full,
            full,
            jax.ShapeDtypeStruct((tokens, width), jnp.bfloat16),
            jax.ShapeDtypeStruct((tokens, 1), jnp.float32),
        ),
        in_specs=[anywhere, anywhere, vmem, vmem, vmem, vmem],
        out_specs=(anywhere, vmem, vmem, vmem, vmem),
        scratch_shapes=[
            pltpu.VMEM((tokens, width), jnp.bfloat16),
            pltpu.VMEM((cores, tokens, 128), jnp.float32),
            pltpu.VMEM((cores, tokens, tokens), jnp.float32),
            *gather_scratch(count),
            pltpu.SemaphoreType.DMA,
            pltpu.SemaphoreType.DMA((cores - 1, 4)),
            pltpu.SemaphoreType.DMA((cores, 4)),
        ],
        compiler_params=pltpu.CompilerParams(
            collective_id=3, has_side_effects=True, vmem_limit_bytes=40 * 1024 * 1024
        ),
        cost_estimate=pl.CostEstimate(
            flops=2 * tokens * tokens * (width + cot_width * cores),
            bytes_accessed=4 * tokens * width + 4 * count * rows * width,
            transcendentals=0,
        ),
    )(weight, layer_input, gain_row, cot, doc_ids[:, None], doc_ids[None, :])


def gather_kernel(
    planes,
    tile_ref,
    weight_hbm,
    cot_ref,
    input_ref,
    gain_ref,
    inv_ref,
    out_ref,
    grad_ref,
    weight_ref,
    weighted_ref,
    inner_ref,
    own_sem,
    send_sems,
    recv_sems,
    weight_sem,
    inner_send,
    inner_recv,
):
    links = Links(planes)
    core, cores = links.mp, links.cores
    width = input_ref.shape[1]
    tile = width // 8
    fetch = pltpu.make_async_copy(weight_hbm, weight_ref, weight_sem)
    fetch.start()
    links.greet(True)

    def inner_copy(slot, step):
        return remote(
            inner_ref.at[slot],
            inner_ref.at[slot],
            inner_send.at[step - 1],
            inner_recv.at[slot],
            links.core_peer(step),
        )

    def project(low, high):
        def at(index, carry):
            columns = pl.ds(pl.multiple_of(index * tile, tile), tile)
            weighted = gain_ref[:, columns] * jnp.dot(
                cot_ref[...], weight_ref[:, columns], preferred_element_type=jnp.float32
            )
            weighted_ref[:, columns] = weighted
            product = weighted * input_ref[:, columns].astype(jnp.float32)
            total = inner_ref[core]
            for lane in range(tile // 128):
                total = total + product[:, lane * 128 : (lane + 1) * 128]
            inner_ref[core] = total
            return carry

        lax.fori_loop(low, high, at, 0)

    def project_first():
        inner_ref[core] = jnp.zeros(inner_ref.shape[1:], jnp.float32)
        fetch.wait()
        project(0, 4)

    def project_rest():
        project(4, 8)
        for step in range(1, cores):
            inner_copy(core, step).start()

    def inner_done():
        for step in range(1, cores):
            inner_copy((core + step) % cores, step).wait_recv()
        total = inner_ref[0]
        for slot in range(1, cores):
            total = total + inner_ref[slot]
        inner = jnp.sum(total, axis=1, keepdims=True) / (width * cores)
        inv = inv_ref[...]
        factor = inv * inv * inv * inner

        def at(index, carry):
            columns = pl.ds(pl.multiple_of(index * tile, tile), tile)
            grad_ref[:, columns] = (
                inv * weighted_ref[:, columns] - input_ref[:, columns].astype(jnp.float32) * factor
            ).astype(jnp.bfloat16)
            return carry

        lax.fori_loop(0, 8, at, 0)

    run_gather(
        links,
        planes,
        tile_ref,
        out_ref,
        own_sem,
        send_sems,
        recv_sems,
        [project_first, project_rest, inner_done],
    )
    for step in range(1, cores):
        inner_copy(core, step).wait_send()


def gather_tiles(tile, count, full_weight, full_cot, layer_input, gain_row, inv_rms):
    rows, width = tile.shape
    tokens = layer_input.shape[0]
    cores = lax.axis_size("mp")
    vmem = pl.BlockSpec(memory_space=pltpu.VMEM)
    anywhere = pl.BlockSpec(memory_space=pl.ANY)
    return pl.pallas_call(
        functools.partial(gather_kernel, count // PLANE),
        out_shape=(
            jax.ShapeDtypeStruct((count, rows, width), tile.dtype),
            jax.ShapeDtypeStruct((tokens, width), jnp.bfloat16),
        ),
        in_specs=[anywhere, anywhere, vmem, vmem, vmem, vmem],
        out_specs=(anywhere, vmem),
        scratch_shapes=[
            pltpu.VMEM(full_weight.shape, full_weight.dtype),
            pltpu.VMEM((tokens, width), jnp.float32),
            pltpu.VMEM((cores, tokens, 128), jnp.float32),
            *gather_scratch(count),
            pltpu.SemaphoreType.DMA,
            pltpu.SemaphoreType.DMA((cores - 1,)),
            pltpu.SemaphoreType.DMA((cores,)),
        ],
        compiler_params=pltpu.CompilerParams(
            collective_id=1, has_side_effects=True, vmem_limit_bytes=48 * 1024 * 1024
        ),
        cost_estimate=pl.CostEstimate(
            flops=2 * tokens * width * full_weight.shape[0],
            bytes_accessed=6 * count * rows * width,
            transcendentals=0,
        ),
    )(tile, full_weight, full_cot, layer_input, gain_row, inv_rms)


def scatter_kernel(
    planes,
    clipped_ref,
    normed_ref,
    seed_ref,
    out_ref,
    part_ref,
    total_ref,
    first_in,
    second_in,
    line_in,
    second_out,
    line_out,
    far_in,
    far_out,
    cross_in,
    cross_out,
    cross_keep,
    last_in,
    last_out,
    send_sems,
    first_sems,
    second_sems,
    line_sems,
    far_send,
    far_sems,
    cross_sems,
):
    links = Links(planes)
    rows, width = out_ref.shape
    half, extra = column_parts(width)
    rest = pl.ds(2 * half, extra)
    block = 16
    links.greet()
    pending = []
    row, col, place = links.row, links.col, links.line
    order = sorted(range(planes), key=lambda line: -max(line, planes - 1 - line))
    first_peer = (links.row_peer(), links.col_peer())
    second_peer = (links.col_peer(), links.row_peer())

    def columns(part):
        return pl.ds(part * half, half)

    def first_copy(line, part):
        if part == 0:
            source = part_ref.at[line, 1 - row, :, :, columns(0)]
        else:
            source = part_ref.at[line, :, 1 - col, :, columns(1)]
        return remote(
            source,
            first_in.at[line, part],
            send_sems.at[line, part, 0],
            first_sems.at[line, part],
            first_peer[part],
        )

    def second_copy(line, part):
        return remote(
            second_out.at[line, part],
            second_in.at[line, part],
            send_sems.at[line, part, 1],
            second_sems.at[line, part],
            second_peer[part],
        )

    def line_copy(line, part, side):
        return remote(
            line_out.at[line, part],
            line_in.at[side, line, part],
            send_sems.at[line, part, 2],
            line_sems.at[side, line, part],
            links.above() if side == 0 else links.below(),
        )

    def make_tiles(line):
        plane_rows = PLANE * rows
        tile = width // 8

        def at(index, carry):
            span = pl.ds(pl.multiple_of(index * tile, tile), tile)
            product = lax.dot_general(
                clipped_ref[:, line * plane_rows : (line + 1) * plane_rows],
                normed_ref[:, span],
                (((0,), (0,)), ((), ())),
                preferred_element_type=jnp.float32,
            )
            for lane in range(PLANE):
                part_ref[line, lane // 2, lane % 2, :, span] = product[
                    lane * rows : (lane + 1) * rows
                ].astype(jnp.bfloat16)
            return carry

        lax.fori_loop(0, 8, at, 0)

    def draw_noise():
        seed = seed_ref[0]
        tile = width // 8
        full_width = width * links.cores
        deep = 8

        def at(index, carry):
            top = pl.multiple_of((index // 8) * deep, deep)
            left = pl.multiple_of((index % 8) * tile, tile)
            row_pos = top + lax.broadcasted_iota(jnp.int32, (deep, tile), 0)
            col_pos = (
                links.mp * width + left + lax.broadcasted_iota(jnp.int32, (deep, tile), 1)
            )
            noise = gauss_noise(seed, row_pos * full_width + col_pos)
            total_ref[pl.ds(top, deep), pl.ds(left, tile)] = NOISE_MULT * CLIP_NORM * noise
            return carry

        lax.fori_loop(0, (rows // deep) * 8, at, 0)

    def send_first(line):
        for part in (0, 1):
            copy = first_copy(line, part)
            copy.start()
            pending.append((None, copy))

    def by_blocks(step):
        def at(index, carry):
            step(pl.ds(pl.multiple_of(index * block, block), block))
            return carry

        lax.fori_loop(0, rows // block, at, 0)

    def send_second(line):
        for part in (0, 1):
            first_copy(line, part).wait_recv()
            give_row, give_col = (row, 1 - col) if part == 0 else (1 - row, col)
            lane = 1 - col if part == 0 else 1 - row

            def step(at):
                second_out[line, part, at, :] = (
                    part_ref[line, give_row, give_col, at, columns(part)].astype(jnp.float32)
                    + first_in[line, part, lane, at, :].astype(jnp.float32)
                ).astype(jnp.bfloat16)

            by_blocks(step)
            copy = second_copy(line, part)
            copy.start()
            pending.append((None, copy))

    def plane_sum(line, part, at):
        lane = col if part == 0 else row
        return (
            part_ref[line, row, col, at, columns(part)].astype(jnp.float32)
            + first_in[line, part, lane, at, :].astype(jnp.float32)
            + second_in[line, part, at, :].astype(jnp.float32)
        )

    def send_line(line):
        for part in (0, 1):
            second_copy(line, part).wait_recv()

            @pl.when(place == line)
            def _():
                def step(at):
                    total_ref[at, columns(part)] += plane_sum(line, part, at)

                by_blocks(step)

            for side, sends, joins in (
                (0, place < line, place > 0),
                (1, place > line, place < planes - 1),
            ):

                @pl.when(jnp.logical_and(sends, joins))
                def _():
                    line_copy(line, part, side).wait_recv()

                    def step(at):
                        line_out[line, part, at, :] = (
                            plane_sum(line, part, at)
                            + line_in[side, line, part, at, :].astype(jnp.float32)
                        ).astype(jnp.bfloat16)

                    by_blocks(step)

                @pl.when(jnp.logical_and(sends, jnp.logical_not(joins)))
                def _():
                    def step(at):
                        line_out[line, part, at, :] = plane_sum(line, part, at).astype(jnp.bfloat16)

                    by_blocks(step)

                copy = line_copy(line, part, side)
                pl.when(sends)(copy.start)
                pending.append((sends, copy))

    def far_sides(line):
        return ((0, place < line, place > 0), (1, place > line, place < planes - 1))

    def far_copy(line, side, source):
        return remote(
            source,
            far_in.at[side, line],
            far_send.at[line],
            far_sems.at[side, line],
            links.above() if side == 0 else links.below(),
        )

    def far_start(line):
        for side, sends, joins in far_sides(line):
            guard = jnp.logical_and(sends, jnp.logical_not(joins))
            copy = far_copy(line, side, part_ref.at[line, :, :, :, rest])
            pl.when(guard)(copy.start)
            pending.append((guard, copy))

    def far_join(line):
        for side, sends, joins in far_sides(line):
            guard = jnp.logical_and(sends, joins)
            copy = far_copy(line, side, far_out.at[line])
            pending.append((guard, copy))

            @pl.when(guard)
            def _():
                copy.wait_recv()

                def step(at):
                    for lane in range(PLANE):
                        up, left = lane // 2, lane % 2
                        far_out[line, up, left, at, :] = (
                            part_ref[line, up, left, at, rest].astype(jnp.float32)
                            + far_in[side, line, up, left, at, :].astype(jnp.float32)
                        ).astype(jnp.bfloat16)

                by_blocks(step)
                copy.start()

    def cross_copy():
        return remote(
            cross_out, cross_in, cross_sems.at[0], cross_sems.at[1], links.col_peer()
        )

    def last_copy():
        return remote(last_out, last_in, cross_sems.at[2], cross_sems.at[3], links.row_peer())

    def far_sum():
        for side, joins in ((0, place > 0), (1, place < planes - 1)):
            pl.when(joins)(far_copy(place, side, far_out.at[place]).wait_recv)

        def step(at):
            for up in range(2):
                for give, left in ((True, 1 - col), (False, col)):
                    total = part_ref[place, up, left, at, rest].astype(jnp.float32)
                    for side, joins in ((0, place > 0), (1, place < planes - 1)):
                        came = far_in[side, place, up, left, at, :].astype(jnp.float32)
                        total = total + jnp.where(joins, came, 0.0)
                    if give:
                        cross_out[up, at, :] = total.astype(jnp.bfloat16)
                    else:
                        cross_keep[up, at, :] = total

        by_blocks(step)
        cross_copy().start()
        pending.append((None, cross_copy()))

    def cross_sum():
        cross_copy().wait_recv()

        def step(at):
            last_out[at, :] = (
                cross_keep[1 - row, at, :] + cross_in[1 - row, at, :].astype(jnp.float32)
            ).astype(jnp.bfloat16)
            total_ref[at, rest] += cross_keep[row, at, :] + cross_in[row, at, :].astype(
                jnp.float32
            )

        by_blocks(step)
        last_copy().start()
        pending.append((None, last_copy()))

    def last_sum():
        last_copy().wait_recv()

        def step(at):
            total_ref[at, rest] += last_in[at, :].astype(jnp.float32)

        by_blocks(step)

    ahead = 2
    for index, line in enumerate(order):
        make_tiles(line)
        if index < ahead:
            send_first(line)
        if extra:
            far_start(line)
    draw_noise()
    joined = 0
    for index, line in enumerate(order):
        send_second(line)
        if index + ahead < planes:
            send_first(order[index + ahead])
        if extra:
            for later in order[joined : joined + 2]:
                far_join(later)
            joined += 2
            if index == planes - 2:
                far_sum()
            if index == planes - 1:
                cross_sum()
        if index > 0:
            send_line(order[index - 1])
    send_line(order[-1])
    if extra:
        last_sum()

    for side, joins in ((0, place > 0), (1, place < planes - 1)):
        for part in (0, 1):

            @pl.when(joins)
            def _():
                line_copy(place, part, side).wait_recv()

                def step(at):
                    total_ref[at, columns(part)] += line_in[side, place, part, at, :].astype(
                        jnp.float32
                    )

                by_blocks(step)

    def finish(at):
        out_ref[at, :] = total_ref[at, :].astype(jnp.bfloat16)

    by_blocks(finish)
    for guard, copy in pending:
        if guard is None:
            copy.wait_send()
        else:
            pl.when(guard)(copy.wait_send)


def scatter_sum(clipped, normed, seed, count):
    planes = count // PLANE
    rows = clipped.shape[1] // count
    width = normed.shape[1]
    vmem = pl.BlockSpec(memory_space=pltpu.VMEM)
    half, extra = column_parts(width)
    spare = max(extra, 128)
    return pl.pallas_call(
        functools.partial(scatter_kernel, planes),
        out_shape=jax.ShapeDtypeStruct((rows, width), jnp.bfloat16),
        in_specs=[vmem, vmem, pl.BlockSpec(memory_space=pltpu.SMEM)],
        out_specs=vmem,
        scratch_shapes=[
            pltpu.VMEM((planes, 2, 2, rows, width), jnp.bfloat16),
            pltpu.VMEM((rows, width), jnp.float32),
            pltpu.VMEM((planes, 2, 2, rows, half), jnp.bfloat16),
            pltpu.VMEM((planes, 2, rows, half), jnp.bfloat16),
            pltpu.VMEM((2, planes, 2, rows, half), jnp.bfloat16),
            pltpu.VMEM((planes, 2, rows, half), jnp.bfloat16),
            pltpu.VMEM((planes, 2, rows, half), jnp.bfloat16),
            pltpu.VMEM((2, planes, 2, 2, rows, spare), jnp.bfloat16),
            pltpu.VMEM((planes, 2, 2, rows, spare), jnp.bfloat16),
            pltpu.VMEM((2, rows, spare), jnp.bfloat16),
            pltpu.VMEM((2, rows, spare), jnp.bfloat16),
            pltpu.VMEM((2, rows, spare), jnp.float32),
            pltpu.VMEM((rows, spare), jnp.bfloat16),
            pltpu.VMEM((rows, spare), jnp.bfloat16),
            pltpu.SemaphoreType.DMA((planes, 2, 3)),
            pltpu.SemaphoreType.DMA((planes, 2)),
            pltpu.SemaphoreType.DMA((planes, 2)),
            pltpu.SemaphoreType.DMA((2, planes, 2)),
            pltpu.SemaphoreType.DMA((planes,)),
            pltpu.SemaphoreType.DMA((2, planes)),
            pltpu.SemaphoreType.DMA((4,)),
        ],
        compiler_params=pltpu.CompilerParams(
            collective_id=2, has_side_effects=True, vmem_limit_bytes=48 * 1024 * 1024
        ),
        cost_estimate=pl.CostEstimate(
            flops=2 * count * rows * width * clipped.shape[0],
            bytes_accessed=8 * count * rows * width,
            transcendentals=0,
        ),
    )(clipped, normed, seed)


def adam_kernel(
    sources_ref,
    filled_ref,
    noisy_ref,
    master_ref,
    first_ref,
    second_ref,
    new_master_ref,
    new_first_ref,
    new_second_ref,
):
    rows, width = master_ref.shape
    filled = filled_ref[pl.program_id(0)] != 0
    tile = min(width, 512)
    across = width // tile

    @pl.when(filled)
    def _():
        def at(index, carry):
            span = (
                pl.ds(pl.multiple_of((index // across) * 16, 16), 16),
                pl.ds(pl.multiple_of((index % across) * tile, tile), tile),
            )
            noisy = noisy_ref[(0,) + span].astype(jnp.float32)
            first_new = BETA_ONE * first_ref[span] + (1.0 - BETA_ONE) * noisy
            second_new = BETA_TWO * second_ref[span] + (1.0 - BETA_TWO) * noisy * noisy
            update = (first_new * (1.0 / (1.0 - BETA_ONE**ADAM_STEP))) / (
                jnp.sqrt(second_new * (1.0 / (1.0 - BETA_TWO**ADAM_STEP))) + ADAM_EPS
            )
            new_master_ref[span] = master_ref[span] - LEARN_RATE * update
            new_first_ref[span] = first_new
            new_second_ref[span] = second_new
            return carry

        lax.fori_loop(0, (rows // 16) * across, at, 0)

    @pl.when(jnp.logical_not(filled))
    def _():
        new_master_ref[...] = master_ref[...]
        new_first_ref[...] = first_ref[...]
        new_second_ref[...] = second_ref[...]


def adam_update(sources, filled, noisy, master, moment_one, moment_two):
    slots = sources.shape[0]
    rows, width = noisy.shape[1:]
    tile = min(width, 2048)
    state = pl.BlockSpec((rows, tile), lambda slot, part, source, full: (slot, part))
    shape = jax.ShapeDtypeStruct(master.shape, master.dtype)
    return pl.pallas_call(
        adam_kernel,
        out_shape=(shape, shape, shape),
        grid_spec=pltpu.PrefetchScalarGridSpec(
            num_scalar_prefetch=2,
            grid=(slots, width // tile),
            in_specs=[
                pl.BlockSpec(
                    (1, rows, tile), lambda slot, part, source, full: (source[slot], 0, part)
                ),
                state,
                state,
                state,
            ],
            out_specs=[state, state, state],
        ),
        compiler_params=pltpu.CompilerParams(vmem_limit_bytes=24 * 1024 * 1024),
        cost_estimate=pl.CostEstimate(
            flops=15 * master.size, bytes_accessed=26 * master.size, transcendentals=0
        ),
    )(sources, filled, noisy, master, moment_one, moment_two)


def body(
    layer_input,
    norm_gain,
    value_weight,
    value_cotangent,
    doc_ids,
    owners,
    noise_seeds,
    master,
    moment_one,
    moment_two,
):
    part_width = layer_input.shape[1]
    group_rows = value_weight.shape[0]
    slot_count = master.shape[0] // group_rows
    cycle_size = lax.axis_size("dp")
    my_group = lax.axis_index("dp")
    gain_row = norm_gain.astype(jnp.float32)[None, :]
    seed_value = noise_seeds[my_group]
    full_weight, full_cot, clipped, normed, inv_rms = gather_and_clip(
        value_weight, layer_input, gain_row, value_cotangent, doc_ids, cycle_size
    )
    full_weight = full_weight.reshape(cycle_size * group_rows, part_width)
    group_ids = jnp.arange(cycle_size, dtype=jnp.int32)
    earlier = group_ids[:, None] > group_ids[None, :]
    same_owner = owners[:, None] == owners[None, :]
    slot_rank = jnp.sum((earlier & same_owner).astype(jnp.int32), axis=1)
    slot_ids = jnp.arange(slot_count, dtype=jnp.int32)
    holds_slot = (owners[None, :] == my_group) & (slot_rank[None, :] == slot_ids[:, None])
    sources = jnp.sum(jnp.where(holds_slot, group_ids[None, :], 0), axis=1)
    filled = jnp.any(holds_slot, axis=1)
    noisy_tile = scatter_sum(clipped, normed, seed_value[None], cycle_size)
    arrived, input_grad = gather_tiles(
        noisy_tile, cycle_size, full_weight, full_cot, layer_input, gain_row, inv_rms
    )
    new_master, new_moment_one, new_moment_two = adam_update(
        sources, filled.astype(jnp.int32), arrived, master, moment_one, moment_two
    )
    return (input_grad, new_master, new_moment_one, new_moment_two)


def solution(mesh):
    in_specs = (
        P("dp", "mp"),
        P("mp"),
        P("dp", "mp"),
        P("dp", "mp"),
        P("dp"),
        P(),
        P(),
        P("dp", "mp"),
        P("dp", "mp"),
        P("dp", "mp"),
    )
    out_specs = (P("dp", "mp"), P("dp", "mp"), P("dp", "mp"), P("dp", "mp"))
    return jax.shard_map(body, mesh=mesh, in_specs=in_specs, out_specs=out_specs, check_vma=False)
```
